32 devices in a mesh: dp: 4 (over y, x), ctx: 8 (over z, core).
Axes of the slice: x: 2, y: 2, z: 4, core: 2. Of those that a mesh axis runs over, the one named last changes fastest.
Arguments:
- hidden_in: bfloat16 [8, 1024, 768], P('dp', 'ctx'), may hold values from -6 to 6
- cotangent: bfloat16 [8, 1024, 768], P('dp', 'ctx'), may hold values from -6 to 6
- w_qkv: bfloat16 [768, 2304], P('dp'), may hold values from -0.3125 to 0.3125
- w_out: bfloat16 [768, 768], P('dp'), may hold values from -0.875 to 0.875
- w_in: bfloat16 [768, 2304], P('dp'), may hold values from -0.21875 to 0.21875
- w_mix: bfloat16 [1152, 768], P('dp'), may hold values from -0.25 to 0.25
- attn_gain: bfloat16 [768], P('dp'), may hold values from 0.5 to 1.5
- mlp_gain: bfloat16 [768], P('dp'), may hold values from 0.5 to 1.5
- segment_ids: int32 [8, 1024], P('dp', 'ctx'), may hold values from 0 to 7, as said below
- positions: int32 [8, 1024], P('dp', 'ctx'), may hold values from 0 to 1023, as said below
Outputs:
- output: bfloat16 [8, 1024, 768], P('dp', 'ctx')
- grad_input: bfloat16 [8, 1024, 768], P('dp', 'ctx')
- grad_w_qkv: float32 [768, 2304], P('dp')
- grad_w_out: float32 [768, 768], P('dp')
- grad_w_in: float32 [768, 2304], P('dp')
- grad_w_mix: float32 [1152, 768], P('dp')
- grad_attn_gain: float32 [768], P('dp')
- grad_mlp_gain: float32 [768], P('dp')
The draws below stay inside these ranges and needn't reach their ends.
Inputs may be any that keep to these rules, and one draw needn't show every extreme that they name: `segment_ids`: along each sequence segment numbers start at 0 and never fall, rising by at most one between neighbouring positions; in each group of 2 sequences of one dp index one sequence is a single document. `positions`: each position's index within its document, counted from 0 at the document's first position.
All inputs are finite; a program needn't handle non-finite values.
Results may differ from the reference program's by a relative error of at most 0.025.
Values may be sent and summed in bfloat16 or wider, within the bound.
A program may use at most 128 MiB of HBM per device.

```python
import jax
import jax.numpy as jnp
from jax import lax

D = 768
HEADS = 12
HEAD_DIM = 64
FF = 1152
SEQS = 2
SEQ_LEN = 1024
SEQUENCES = 8


segment_top = 7


def packing(key):
    mark_key = jax.random.fold_in(key, 101)
    pick_key = jax.random.fold_in(key, 102)
    places = jnp.arange(SEQ_LEN, dtype=jnp.int32)[None, :]
    rolled = jax.random.randint(mark_key, (SEQUENCES, SEQ_LEN), 0, max(SEQ_LEN // 4, 2))
    boundary = jnp.where((rolled == 0) & (places > 0), 1, 0).astype(jnp.int32)
    chosen = jax.random.randint(pick_key, (SEQUENCES // SEQS,), 0, SEQS)
    rows = jnp.arange(SEQUENCES, dtype=jnp.int32)
    forced_row = rows == (chosen[0] + 1) % SEQS
    fixed_marks = jnp.where((places % (SEQ_LEN // 8) == 0) & (places > 0), 1, 0).astype(jnp.int32)
    boundary = jnp.where(forced_row[:, None], jnp.maximum(boundary, fixed_marks), boundary)
    single = rows % SEQS == jnp.repeat(chosen, SEQS)
    boundary = jnp.where(single[:, None], 0, boundary)
    segments = jnp.minimum(jnp.cumsum(boundary, axis=1), segment_top).astype(jnp.int32)
    earlier = jnp.concatenate([jnp.zeros((SEQUENCES, 1), jnp.int32), segments[:, :-1]], axis=1)
    kept = (segments - earlier).astype(jnp.int32)
    starts = lax.cummax(jnp.where(kept == 1, places, 0), axis=1)
    return (segments, (places - starts).astype(jnp.int32))


def draw_segment_ids(key, part):
    shared = packing(key)
    return shared[0]


def draw_positions(key, part):
    shared = packing(key)
    return shared[1]


def block_scale(stream_key, shape, shards, smallest, largest):
    loudness = 1.0
    for dim, shards_of in shards:
        draws = jax.random.uniform(jax.random.fold_in(jax.random.fold_in(stream_key, 6), dim), (shards_of,), jnp.float32, smallest / len(shards), largest / len(shards))
        loudness = loudness * jnp.repeat(jnp.exp(draws), shape[dim] // shards_of).reshape((-1,) + (1,) * (len(shape) - 1 - dim))
    return loudness


def gaussian(stream_key, dims, spread, bound, split=(), kind=jnp.bfloat16):
    drawn = spread * jax.random.normal(stream_key, dims, jnp.float32)
    if split:
        drawn = drawn * block_scale(stream_key, dims, split, -0.22, 0.18)
    return jnp.clip(drawn, -bound, bound).astype(kind)


def setup_inputs(seed: int = 0) -> dict:
    seeds = jax.random.split(jax.random.key(seed), 11)
    hidden_in = gaussian(seeds[0], (SEQUENCES, SEQ_LEN, D), 1.0, 6.0, ((0, 4), (1, 8)))
    cotangent = gaussian(seeds[1], (SEQUENCES, SEQ_LEN, D), 1.0, 6.0, ((0, 4), (1, 8)))
    w_qkv = gaussian(seeds[2], (D, 3 * D), (D // 2) ** -0.5, 0.3125, ((0, 4),))
    w_out = gaussian(seeds[3], (D, D), (D // 16) ** -0.5, 0.875, ((0, 4),))
    w_in = gaussian(seeds[4], (D, 2 * FF), D ** -0.5, 0.21875, ((0, 4),))
    w_mix = gaussian(seeds[5], (FF, D), (FF // 2) ** -0.5, 0.25, ((0, 4),))
    attn_gain = jnp.clip(1.0 + 0.1 * jax.random.normal(seeds[6], (D,), jnp.float32), 0.5, 1.5).astype(jnp.bfloat16)
    mlp_gain = jnp.clip(1.0 + 0.1 * jax.random.normal(seeds[7], (D,), jnp.float32), 0.5, 1.5).astype(jnp.bfloat16)
    segment_ids = draw_segment_ids(jax.random.fold_in(seeds[10], 71), 0)
    positions = draw_positions(jax.random.fold_in(seeds[10], 71), 0)
    return dict(hidden_in=hidden_in, cotangent=cotangent, w_qkv=w_qkv, w_out=w_out, w_in=w_in, w_mix=w_mix, attn_gain=attn_gain, mlp_gain=mlp_gain, segment_ids=segment_ids, positions=positions)


epsilon = 1e-05
rope_base = 160000.0
masked_score = -1e+30
highest = lax.Precision.HIGHEST

@jax.custom_vjp
def low(v):
    return lax.optimization_barrier(v.astype(jnp.bfloat16)).astype(jnp.float32)

@jax.custom_vjp
def low_back(v):
    return v

def low_keep(v):
    return (low(v), None)

def low_pass(kept, grad):
    return (grad,)

def back_keep(v):
    return (v, None)

def back_low(kept, grad):
    return (low(grad),)
low.defvjp(low_keep, low_pass)
low_back.defvjp(back_keep, back_low)

def norm_gain(values, gain_row):
    row_mean = lax.optimization_barrier(jnp.mean(values, -1, keepdims=True))
    centred = values - row_mean
    return centred * lax.rsqrt(lax.optimization_barrier(jnp.mean(centred * centred, -1, keepdims=True)) + epsilon) * gain_row

def rotate(values, positions, direction):
    half_width = values.shape[-1] // 2
    frequency = rope_base ** (-2.0 * jnp.arange(half_width, dtype=jnp.float32) / values.shape[-1])
    angles = positions.astype(jnp.float32)[..., None] * frequency
    cosine = jnp.cos(angles)[..., None, :]
    sine_part = direction * jnp.sin(angles)[..., None, :]
    first_half = values[..., :half_width]
    second = values[..., half_width:]
    return jnp.concatenate([first_half * cosine - second * sine_part, second * cosine + first_half * sine_part], -1)

def sequence_layer(tokens, w_qkv, w_out, w_in, w_mix, gain_attn, gain_mlp, segments, places):
    length = tokens.shape[0]
    score_scale = HEAD_DIM ** (-0.5)
    normed_low = low(norm_gain(tokens, gain_attn))
    projected = low_back(jnp.dot(normed_low, w_qkv, precision=highest)).reshape(length, 3, HEADS, HEAD_DIM)
    query_heads = low(rotate(projected[:, 0], places, 1.0))
    key_heads = low(rotate(projected[:, 1], places, 1.0))
    value_heads = low(projected[:, 2])
    allowed = segments[:, None] == segments[None, :]

    def one_head(head_parts):
        query_head, key_head, value_head = head_parts
        scores = low_back(jnp.dot(query_head, key_head.T, precision=highest) * score_scale)
        chances = low(jax.nn.softmax(jnp.where(allowed, scores, masked_score), axis=-1))
        return jnp.dot(chances, value_head, precision=highest)
    mixed = lax.map(jax.checkpoint(one_head), (jnp.moveaxis(query_heads, 1, 0), jnp.moveaxis(key_heads, 1, 0), jnp.moveaxis(value_heads, 1, 0)))
    attention = low_back(low(jnp.moveaxis(mixed, 0, 1).reshape(length, HEADS * HEAD_DIM)))
    residual = tokens + low_back(jnp.dot(attention, w_out, precision=highest))
    normed_mlp = low(norm_gain(residual, gain_mlp))
    wide_proj = low_back(jnp.dot(normed_mlp, w_in, precision=highest))
    activated = low(jax.nn.gelu(wide_proj[:, :FF], approximate=False) * wide_proj[:, FF:])
    return residual + jnp.dot(activated, w_mix, precision=highest)

def reference(hidden_in, cotangent, w_qkv, w_out, w_in, w_mix, attn_gain, mlp_gain, segment_ids, positions):
    weights = (w_qkv.astype(jnp.float32), w_out.astype(jnp.float32), w_in.astype(jnp.float32), w_mix.astype(jnp.float32), attn_gain.astype(jnp.float32), mlp_gain.astype(jnp.float32))

    def one_sequence(totals, members):
        tokens, grad_out, segments, places = members

        def layer_fn(tok_rows, first_w, second_w, third_w, fourth_w, gain_one, gain_two):
            return sequence_layer(tok_rows, first_w, second_w, third_w, fourth_w, gain_one, gain_two, segments, places)
        output, pullback = jax.vjp(layer_fn, tokens.astype(jnp.float32), weights[0], weights[1], weights[2], weights[3], weights[4], weights[5])
        gradients = pullback(grad_out.astype(jnp.float32))
        totals = tuple((total_sum + grad_one for total_sum, grad_one in zip(totals, gradients[1:])))
        return (totals, (output.astype(jnp.bfloat16), gradients[0].astype(jnp.bfloat16)))
    zero_grads = tuple((jnp.zeros(weight.shape, jnp.float32) for weight in weights))
    totals, (outputs, grad_inputs) = lax.scan(one_sequence, zero_grads, (hidden_in, cotangent, segment_ids, positions))
    return (outputs, grad_inputs, totals[0], totals[1], totals[2], totals[3], totals[4], totals[5])
```

```python
import jax
import jax.numpy as jnp
from jax import lax
from jax.experimental import pallas as pl
from jax.experimental.pallas import tpu as pltpu
from jax.sharding import PartitionSpec as P

HEADS = 12
HEAD_DIM = 64


epsilon = 1e-05
rope_base = 160000.0
masked_score = -1e30


def norm_gain(values, gain_row):
    row_mean = jnp.mean(values, -1, keepdims=True)
    centred = values - row_mean
    return centred * lax.rsqrt(jnp.mean(centred * centred, -1, keepdims=True) + epsilon) * gain_row


def rotate(values, positions, direction):
    half_width = values.shape[-1] // 2
    frequency = rope_base ** (-2.0 * jnp.arange(half_width, dtype=jnp.float32) / values.shape[-1])
    angles = positions.astype(jnp.float32)[..., None] * frequency
    cosine = jnp.cos(angles)[..., None, :]
    sine_part = direction * jnp.sin(angles)[..., None, :]
    first_half = values[..., :half_width]
    second = values[..., half_width:]
    return jnp.concatenate(
        [first_half * cosine - second * sine_part, second * cosine + first_half * sine_part], -1
    )


def geglu(projected):
    half_width = projected.shape[-1] // 2
    return jax.nn.gelu(projected[..., :half_width], approximate=False) * projected[..., half_width:]


def inner(left_arg, right_arg):
    return lax.dot_general(
        left_arg, right_arg, (((0,), (0,)), ((), ())), preferred_element_type=jnp.float32
    )


def times_back(left_arg, right_arg):
    return lax.dot_general(
        left_arg, right_arg, (((1,), (1,)), ((), ())), preferred_element_type=jnp.float32
    )


def heads_view(values):
    return values.reshape(values.shape[:2] + (HEADS, HEAD_DIM))


def same_doc(query_docs, key_docs):
    return query_docs[:, None, :, None] == key_docs[:, None, None, :]


def blockwise(stepper, initial, arrays, block_len):
    key_count = arrays[0].shape[1]
    block_count = key_count // block_len
    pieces = tuple(
        (
            jnp.moveaxis(
                member.reshape(member.shape[:1] + (block_count, block_len) + member.shape[2:]), 1, 0
            )
            for member in arrays
        )
    )
    return lax.scan(lambda running, members: (stepper(running, members), None), initial, pieces)[0]


def long_body(
    hidden_in, cotangent, w_qkv, w_out, w_in, w_mix, attn_gain, mlp_gain, segment_ids, positions
):
    seq_count, local_len, model_width = hidden_in.shape
    row_count = seq_count * local_len
    score_scale = HEAD_DIM ** (-0.5)
    full_qkv, full_out, full_in, full_mix, gain_attn, gain_mlp = (
        lax.all_gather(w_qkv, "dp", axis=0, tiled=True),
        lax.all_gather(w_out, "dp", axis=0, tiled=True),
        lax.all_gather(w_in, "dp", axis=0, tiled=True),
        lax.all_gather(w_mix, "dp", axis=0, tiled=True),
        lax.all_gather(attn_gain, "dp", axis=0, tiled=True),
        lax.all_gather(mlp_gain, "dp", axis=0, tiled=True),
    )
    all_segments = lax.all_gather(segment_ids, "ctx", axis=1, tiled=True)
    inputs = hidden_in.astype(jnp.float32).reshape(row_count, model_width)
    normed_attn, attn_norm_back = jax.vjp(norm_gain, inputs, gain_attn.astype(jnp.float32))
    normed_low = normed_attn.astype(jnp.bfloat16)
    projected = jnp.dot(normed_low, full_qkv, preferred_element_type=jnp.float32).reshape(
        seq_count, local_len, 3, HEADS, HEAD_DIM
    )
    query_heads = rotate(projected[:, :, 0], positions, 1.0).astype(jnp.bfloat16)
    key_low = (
        rotate(projected[:, :, 1], positions, 1.0)
        .astype(jnp.bfloat16)
        .reshape(seq_count, local_len, model_width)
    )
    value_low = projected[:, :, 2].astype(jnp.bfloat16).reshape(seq_count, local_len, model_width)
    key_heads = heads_view(key_low)
    value_heads = heads_view(value_low)

    def attend_block(running, members):
        row_max, row_total, weighted = running
        key_part, value_part, key_docs = members
        scores = (
            jnp.einsum(
                "sqhd,skhd->shqk",
                query_heads,
                heads_view(key_part),
                preferred_element_type=jnp.float32,
            )
            * score_scale
        )
        allowed = same_doc(segment_ids, key_docs)
        newest = jnp.maximum(row_max, jnp.max(jnp.where(allowed, scores, masked_score), -1))
        weights = jnp.where(allowed, jnp.exp(scores - newest[..., None]), 0.0)
        factor = jnp.exp(row_max - newest)
        update = jnp.einsum(
            "shqk,skhd->sqhd",
            weights.astype(jnp.bfloat16),
            heads_view(value_part),
            preferred_element_type=jnp.float32,
        )
        return (
            newest,
            row_total * factor + jnp.sum(weights, -1),
            weighted * jnp.moveaxis(factor, 1, 2)[..., None] + update,
        )

    stat_shape = (seq_count, HEADS, local_len)
    head_shape = (seq_count, local_len, HEADS, HEAD_DIM)
    start_state = (
        jnp.full(stat_shape, masked_score, jnp.float32),
        jnp.zeros(stat_shape, jnp.float32),
        jnp.zeros(head_shape, jnp.float32),
    )
    arriving = (
        lax.all_gather(key_low, "ctx", axis=1, tiled=True),
        lax.all_gather(value_low, "ctx", axis=1, tiled=True),
    )
    key_docs = all_segments
    row_max, row_total, weighted = blockwise(
        attend_block, start_state, (arriving[0], arriving[1], key_docs), local_len
    )
    attention = (weighted / jnp.moveaxis(row_total, 1, 2)[..., None]).reshape(
        row_count, model_width
    )
    log_total = jnp.moveaxis(row_max + jnp.log(row_total), 1, 2)
    attn_low = attention.astype(jnp.bfloat16)
    residual = inputs + jnp.dot(attn_low, full_out, preferred_element_type=jnp.float32)
    normed_mlp, mlp_norm_back = jax.vjp(norm_gain, residual, gain_mlp.astype(jnp.float32))
    mlp_low = normed_mlp.astype(jnp.bfloat16)
    wide_proj = jnp.dot(mlp_low, full_in, preferred_element_type=jnp.float32)
    activated, geglu_back = jax.vjp(geglu, wide_proj)
    act_low = activated.astype(jnp.bfloat16)
    output = residual + jnp.dot(act_low, full_mix, preferred_element_type=jnp.float32)
    grad_out = cotangent.reshape(row_count, model_width)
    grad_mix = inner(act_low, grad_out)
    grad_wide = geglu_back(times_back(grad_out, full_mix))[0].astype(jnp.bfloat16)
    grad_in = inner(mlp_low, grad_wide)
    grad_norm_in, grad_gain_mlp = mlp_norm_back(times_back(grad_wide, full_in))
    grad_resid = grad_out.astype(jnp.float32) + grad_norm_in
    grad_branch = grad_resid.astype(jnp.bfloat16)
    grad_attn_out = inner(attn_low, grad_branch)
    grad_heads = times_back(grad_branch, full_out).astype(jnp.bfloat16)
    grad_view = grad_heads.reshape(head_shape)
    offsets = jnp.sum(grad_view.astype(jnp.float32) * attention.reshape(head_shape), -1)
    all_logs, all_offsets = (
        lax.all_gather(log_total, "ctx", axis=1, tiled=True),
        lax.all_gather(offsets, "ctx", axis=1, tiled=True),
    )
    own_logs = jnp.moveaxis(log_total, 2, 1)[..., None]
    own_offsets = jnp.moveaxis(offsets, 2, 1)[..., None]
    grad_rows = grad_heads.reshape(seq_count, local_len, model_width)
    query_low = query_heads.reshape(seq_count, local_len, model_width)

    def query_terms(key_part, value_part, key_docs):
        scores = (
            jnp.einsum(
                "sqhd,skhd->shqk",
                query_heads,
                heads_view(key_part),
                preferred_element_type=jnp.float32,
            )
            * score_scale
        )
        allowed = same_doc(segment_ids, key_docs)
        attn_probs = jnp.where(allowed, jnp.exp(scores - own_logs), 0.0)
        grad_probs = jnp.einsum(
            "sqhd,skhd->shqk", grad_view, heads_view(value_part), preferred_element_type=jnp.float32
        )
        grad_scores = (attn_probs * (grad_probs - own_offsets)).astype(jnp.bfloat16)
        return (
            jnp.einsum(
                "shqk,skhd->sqhd",
                grad_scores,
                heads_view(key_part),
                preferred_element_type=jnp.float32,
            )
            * score_scale
        )

    def key_terms(query_part, grad_part, query_docs, logs_part, offsets_part):
        query_view = heads_view(query_part)
        grad_part_view = heads_view(grad_part)
        scores = (
            jnp.einsum("sqhd,skhd->shqk", query_view, key_heads, preferred_element_type=jnp.float32)
            * score_scale
        )
        allowed = same_doc(query_docs, segment_ids)
        attn_probs = jnp.where(
            allowed, jnp.exp(scores - jnp.moveaxis(logs_part, 2, 1)[..., None]), 0.0
        )
        grad_value = jnp.einsum(
            "shqk,sqhd->skhd",
            attn_probs.astype(jnp.bfloat16),
            grad_part_view,
            preferred_element_type=jnp.float32,
        )
        grad_probs = jnp.einsum(
            "sqhd,skhd->shqk", grad_part_view, value_heads, preferred_element_type=jnp.float32
        )
        grad_scores = (
            attn_probs * (grad_probs - jnp.moveaxis(offsets_part, 2, 1)[..., None])
        ).astype(jnp.bfloat16)
        grad_key = (
            jnp.einsum(
                "shqk,sqhd->skhd", grad_scores, query_view, preferred_element_type=jnp.float32
            )
            * score_scale
        )
        return (grad_key, grad_value)

    zero_heads = jnp.zeros(head_shape, jnp.float32)

    def query_block(running, members):
        return running + query_terms(members[0], members[1], members[2])

    arriving = (
        lax.all_gather(key_low, "ctx", axis=1, tiled=True),
        lax.all_gather(value_low, "ctx", axis=1, tiled=True),
    )
    grad_query = blockwise(
        query_block, zero_heads, (arriving[0], arriving[1], all_segments), local_len
    )

    def key_block(running, members):
        grad_key, grad_value = key_terms(members[0], members[1], members[2], members[3], members[4])
        return (running[0] + grad_key, running[1] + grad_value)

    grad_key, grad_value = blockwise(
        key_block,
        (zero_heads, zero_heads),
        (
            lax.all_gather(query_low, "ctx", axis=1, tiled=True),
            lax.all_gather(grad_rows, "ctx", axis=1, tiled=True),
        )
        + (all_segments, all_logs, all_offsets),
        local_len,
    )
    grad_qkv = (
        jnp.stack(
            [rotate(grad_query, positions, -1.0), rotate(grad_key, positions, -1.0), grad_value], 2
        )
        .reshape(row_count, 3 * model_width)
        .astype(jnp.bfloat16)
    )
    grad_qkv_w = inner(normed_low, grad_qkv)
    grad_norm_attn, grad_gain_attn = attn_norm_back(times_back(grad_qkv, full_qkv))
    grad_hidden = (grad_resid + grad_norm_attn).astype(jnp.bfloat16).reshape(hidden_in.shape)
    grad_terms = (grad_qkv_w, grad_attn_out, grad_in, grad_mix, grad_gain_attn, grad_gain_mlp)
    summed = (
        lax.psum(grad_terms[0].astype(jnp.bfloat16), "ctx").astype(jnp.float32),
        lax.psum(grad_terms[1].astype(jnp.bfloat16), "ctx").astype(jnp.float32),
        lax.psum(grad_terms[2].astype(jnp.bfloat16), "ctx").astype(jnp.float32),
        lax.psum(grad_terms[3].astype(jnp.bfloat16), "ctx").astype(jnp.float32),
        lax.psum(grad_terms[4].astype(jnp.bfloat16), "ctx").astype(jnp.float32),
        lax.psum(grad_terms[5].astype(jnp.bfloat16), "ctx").astype(jnp.float32),
    )
    owner_grads = (
        lax.psum_scatter(
            summed[0].astype(jnp.bfloat16), "dp", scatter_dimension=0, tiled=True
        ).astype(jnp.float32),
        lax.psum_scatter(
            summed[1].astype(jnp.bfloat16), "dp", scatter_dimension=0, tiled=True
        ).astype(jnp.float32),
        lax.psum_scatter(
            summed[2].astype(jnp.bfloat16), "dp", scatter_dimension=0, tiled=True
        ).astype(jnp.float32),
        lax.psum_scatter(
            summed[3].astype(jnp.bfloat16), "dp", scatter_dimension=0, tiled=True
        ).astype(jnp.float32),
        lax.psum_scatter(
            summed[4].astype(jnp.bfloat16), "dp", scatter_dimension=0, tiled=True
        ).astype(jnp.float32),
        lax.psum_scatter(
            summed[5].astype(jnp.bfloat16), "dp", scatter_dimension=0, tiled=True
        ).astype(jnp.float32),
    )
    return (
        output.astype(jnp.bfloat16).reshape(hidden_in.shape),
        grad_hidden,
        owner_grads[0],
        owner_grads[1],
        owner_grads[2],
        owner_grads[3],
        owner_grads[4],
        owner_grads[5],
    )

PAIR = 2 * HEAD_DIM
VMEM_LIMIT = 56 * 1024 * 1024


def dot_nn(left, right):
    return jnp.dot(left, right, preferred_element_type=jnp.float32)


def turn(values, cosine, sine):
    lane = lax.broadcasted_iota(jnp.int32, values.shape, 1)
    half = HEAD_DIM // 2
    partner = jnp.where(
        lane % HEAD_DIM < half,
        pltpu.roll(values, PAIR - half, 1),
        pltpu.roll(values, half, 1),
    )
    return values * cosine + partner * sine


def head_lanes(shape, head):
    lane = lax.broadcasted_iota(jnp.int32, shape, 1)
    return lane // HEAD_DIM == head


def forward_kernel(
    seqs, x_all, x_own, wq, wk, wv, cos_all, sin_all, cos_own, sin_own, seg_col, seg_row,
    q_out, k_out, v_out, attn_out, log_out,
):
    scale = HEAD_DIM ** (-0.5)
    q_out[...] = turn(dot_nn(x_own[...], wq[...]), cos_own[...], sin_own[...]).astype(jnp.bfloat16)
    k_out[...] = turn(dot_nn(x_all[...], wk[...]), cos_all[...], sin_all[...]).astype(jnp.bfloat16)
    v_out[...] = dot_nn(x_all[...], wv[...]).astype(jnp.bfloat16)
    local = x_own.shape[0] // seqs
    length = x_all.shape[0] // seqs
    for seq in range(seqs):
        own = pl.ds(seq * local, local)
        whole = pl.ds(seq * length, length)
        allowed = seg_col[own, 0:1] == seg_row[seq : seq + 1, :]
        query, key, value = q_out[own, :], k_out[whole, :], v_out[whole, :]
        first = head_lanes(query.shape, 0)
        parts, logs = [], []
        for head in range(2):
            picked = jnp.where(head_lanes(query.shape, head), query * scale, 0).astype(jnp.bfloat16)
            scores = jnp.where(allowed, times_back(picked, key), masked_score)
            top = jnp.max(scores, -1, keepdims=True)
            weights = jnp.exp(scores - top)
            total = jnp.sum(weights, -1, keepdims=True)
            parts.append(dot_nn(weights.astype(jnp.bfloat16), value) / total)
            logs.append(top + jnp.log(total))
        attn_out[own, :] = jnp.where(first, parts[0], parts[1])
        log_out[own, :] = jnp.where(first, logs[0], logs[1])


def backward_kernel(
    seqs, x_all, x_own, wq, wk, wv, cos_all, sin_all, cos_own, sin_own, seg_col, seg_row,
    q_own, k_own, v_own, k_all, v_all, g_own, g_all, attn, logs, log_row, off_row,
    dw_out, r_out, q_all, gp,
):
    scale = HEAD_DIM ** (-0.5)
    q_all[...] = turn(dot_nn(x_all[...], wq[...]), cos_all[...], sin_all[...]).astype(jnp.bfloat16)
    local = x_own.shape[0] // seqs
    length = x_all.shape[0] // seqs
    for seq in range(seqs):
        own = pl.ds(seq * local, local)
        whole = pl.ds(seq * length, length)
        allowed = seg_col[own, 0:1] == seg_row[seq : seq + 1, :]
        query, key, value, grad = q_own[own, :], k_own[own, :], v_own[own, :], g_own[own, :]
        query_w, key_w, value_w, grad_w = q_all[whole, :], k_all[whole, :], v_all[whole, :], g_all[whole, :]
        first = head_lanes(query.shape, 0)
        weighted = grad.astype(jnp.float32) * attn[own, :]
        dq, dk, dv = [], [], []
        for head in range(2):
            mine = head_lanes(query.shape, head)
            offset = jnp.sum(jnp.where(mine, weighted, 0.0), -1, keepdims=True)
            log = logs[own, head * HEAD_DIM : head * HEAD_DIM + 1]
            picked = jnp.where(mine, query * scale, 0).astype(jnp.bfloat16)
            scores = times_back(picked, key_w)
            probs = jnp.exp(jnp.where(allowed, scores - log, masked_score))
            g_probs = times_back(jnp.where(mine, grad, 0).astype(jnp.bfloat16), value_w)
            g_scores = (probs * (g_probs - offset)).astype(jnp.bfloat16)
            dq.append(dot_nn(g_scores, key_w))
            row = 2 * seq + head
            picked = jnp.where(mine, key * scale, 0).astype(jnp.bfloat16)
            scores = times_back(picked, query_w)
            probs = jnp.exp(jnp.where(allowed, scores - log_row[0, row : row + 1, :], masked_score))
            dv.append(dot_nn(probs.astype(jnp.bfloat16), grad_w))
            g_probs = times_back(jnp.where(mine, value, 0).astype(jnp.bfloat16), grad_w)
            g_scores = (probs * (g_probs - off_row[0, row : row + 1, :])).astype(jnp.bfloat16)
            dk.append(dot_nn(g_scores, query_w))
        cosine, sine = cos_own[own, :], -sin_own[own, :]
        gp[0, own, :] = turn(jnp.where(first, dq[0], dq[1]) * scale, cosine, sine).astype(jnp.bfloat16)
        gp[1, own, :] = turn(jnp.where(first, dk[0], dk[1]) * scale, cosine, sine).astype(jnp.bfloat16)
        gp[2, own, :] = jnp.where(first, dv[0], dv[1]).astype(jnp.bfloat16)
    for part in range(3):
        dw_out[part] = inner(x_own[...], gp[part]).astype(jnp.bfloat16)
    back = times_back(gp[0], wq[...]) + times_back(gp[1], wk[...]) + times_back(gp[2], wv[...])

    @pl.when(pl.program_id(0) == 0)
    def _():
        r_out[...] = back

    @pl.when(pl.program_id(0) > 0)
    def _():
        r_out[...] += back


MESH = pl.DeviceIdType.MESH


def partner_of(index, step):
    low = (index % 2 + step % 2) % 2
    high = (index // 2 + step // 2) % 2
    return high * 2 + low


def meet(peers):
    barrier = pltpu.get_barrier_semaphore()
    for peer in peers:
        pl.semaphore_signal(barrier, inc=1, device_id=peer, device_id_type=MESH)
    pl.semaphore_wait(barrier, len(peers))


def neighbours():
    dp, ctx = lax.axis_index("dp"), lax.axis_index("ctx")
    chip, core = ctx // 2, ctx % 2
    across = [(partner_of(dp, step), ctx) for step in (1, 2, 3)]
    along = [(dp, partner_of(chip, step) * 2 + core) for step in (1, 2, 3)]
    return dp, ctx, across, along, (dp, chip * 2 + 1 - core)


def gather_kernel(n_dp, n_ctx, *refs):
    count = n_dp + n_ctx
    ins, outs = refs[:count], refs[count : 2 * count]
    own_sem, send, recv, pass_send, pass_recv = refs[2 * count :]
    dp, ctx, across, along, sibling = neighbours()
    core = ctx % 2
    meet((across if n_dp else []) + along + [sibling])

    def part(which, place_dp, place_ctx):
        out, block = outs[which], ins[which].shape
        if which < n_dp:
            half = block[0] // 2
            return out.at[pl.ds(place_dp * block[0] + core * half, half)]
        return out.at[:, pl.ds(place_ctx * block[1], block[1])]

    jobs, local = [], []
    for which in range(count):
        rows = ins[which].shape[0]
        peers = across if which < n_dp else along
        if which < n_dp:
            source = ins[which].at[pl.ds(core * (rows // 2), rows // 2)]
            own = outs[which].at[pl.ds(dp * rows, rows)]
        else:
            source, own = ins[which], part(which, dp, ctx)
        keep = pltpu.make_async_copy(ins[which], own, own_sem.at[which])
        keep.start()
        local.append(keep)
        for step in range(3):
            job = pltpu.make_async_remote_copy(
                source, part(which, dp, ctx), send.at[which, step], recv.at[which, step],
                device_id=peers[step], device_id_type=MESH,
            )
            job.start()
            jobs.append((which, step, peers[step], job))
    passed = []
    for which in range(n_dp, count):
        job = pltpu.make_async_remote_copy(
            ins[which], part(which, dp, ctx), pass_send.at[which, 3], pass_recv.at[which, 3],
            device_id=sibling, device_id_type=MESH,
        )
        job.start()
        passed.append(job)
    for which, step, peer, job in jobs:
        job.wait_recv()
        landed = part(which, peer[0], peer[1])
        onward = pltpu.make_async_remote_copy(
            landed, landed, pass_send.at[which, step], pass_recv.at[which, step],
            device_id=sibling, device_id_type=MESH,
        )
        onward.start()
        passed.append(onward)
    for keep in local:
        keep.wait()
    for job in jobs:
        job[3].wait_send()
    for job in passed:
        job.wait()


def gather(dp_arrays, ctx_arrays, collective):
    arrays = tuple(dp_arrays) + tuple(ctx_arrays)
    n_dp, count = len(dp_arrays), len(arrays)
    dp_size, ctx_size = lax.axis_size("dp"), lax.axis_size("ctx")
    shapes = [(a.shape[0] * dp_size,) + a.shape[1:] for a in dp_arrays]
    shapes += [(a.shape[0], a.shape[1] * ctx_size) + a.shape[2:] for a in ctx_arrays]
    dma = pltpu.SemaphoreType.DMA
    return pl.pallas_call(
        lambda *refs: gather_kernel(n_dp, count - n_dp, *refs),
        in_specs=[pl.BlockSpec(memory_space=pl.ANY)] * count,
        out_specs=[pl.BlockSpec(memory_space=pl.ANY)] * count,
        out_shape=[jax.ShapeDtypeStruct(shape, a.dtype) for shape, a in zip(shapes, arrays)],
        scratch_shapes=[dma((count,)), dma((count, 3)), dma((count, 3)), dma((count, 4)), dma((count, 4))],
        compiler_params=pltpu.CompilerParams(collective_id=collective, has_side_effects=True),
    )(*arrays)


def reduce_kernel(
    terms, out, from_core, summed, from_dp, reduced, from_ctx, final,
    core_send, core_recv, dp_send, dp_recv, ctx_send, ctx_recv, spread_send, spread_recv, last,
):
    dp, ctx, across, along, sibling = neighbours()
    chip, core = ctx // 2, ctx % 2
    half, width = reduced.shape
    piece = half // 4
    meet(across + along + [sibling])

    def add(target, sources):
        def chunk(index, carry):
            rows = pl.ds(pl.multiple_of(index * 16, 16), 16)
            value = sources[0][rows, :].astype(jnp.float32)
            for source in sources[1:]:
                value = value + source[rows, :].astype(jnp.float32)
            target[rows, :] = value.astype(jnp.bfloat16)
            return carry

        lax.fori_loop(0, target.shape[0] // 16, chunk, 0)

    swaps = []
    for step in (1, 2, 3, 0):
        owner = partner_of(dp, step)
        swap = pltpu.make_async_remote_copy(
            terms.at[owner, pl.ds((1 - core) * half, half)], from_core.at[step],
            core_send.at[step], core_recv.at[step], device_id=sibling, device_id_type=MESH,
        )
        swap.start()
        swaps.append(swap)
    moves = []
    for step, swap in zip((1, 2, 3, 0), swaps):
        swap.wait_recv()
        owner = partner_of(dp, step)
        add(summed.at[step], [terms.at[owner, pl.ds(core * half, half)], from_core.at[step]])
        if step:
            move = pltpu.make_async_remote_copy(
                summed.at[step], from_dp.at[step - 1], dp_send.at[step - 1], dp_recv.at[step - 1],
                device_id=across[step - 1], device_id_type=MESH,
            )
            move.start()
            moves.append(move)
    for move in moves:
        move.wait_recv()
    add(reduced, [summed.at[0], from_dp.at[0], from_dp.at[1], from_dp.at[2]])
    for step in range(3):
        target = along[step][1] // 2
        move = pltpu.make_async_remote_copy(
            reduced.at[pl.ds(target * piece, piece)], from_ctx.at[step], ctx_send.at[step], ctx_recv.at[step],
            device_id=along[step], device_id_type=MESH,
        )
        move.start()
        moves.append(move)
    for move in moves[3:]:
        move.wait_recv()
    mine = pl.ds(core * half + chip * piece, piece)
    add(final, [reduced.at[pl.ds(chip * piece, piece)], from_ctx.at[0], from_ctx.at[1], from_ctx.at[2]])
    spread = []
    for step in range(3):
        move = pltpu.make_async_remote_copy(
            final, out.at[mine], spread_send.at[step], spread_recv.at[step],
            device_id=along[step], device_id_type=MESH,
        )
        move.start()
        spread.append(move)
    keep = pltpu.make_async_copy(final, out.at[mine], last.at[0])
    keep.start()
    keep.wait()
    for move in spread:
        move.wait_recv()
    whole = pl.ds(core * half, half)
    share = pltpu.make_async_remote_copy(
        out.at[whole], out.at[whole], last.at[1], last.at[2], device_id=sibling, device_id_type=MESH
    )
    share.start()
    for move in swaps + moves + spread:
        move.wait_send()
    share.wait()


def reduce_terms(terms, collective):
    _, rows, width = terms.shape
    half = rows // 2
    bf, dma = jnp.bfloat16, pltpu.SemaphoreType.DMA
    return pl.pallas_call(
        reduce_kernel,
        in_specs=[pl.BlockSpec(memory_space=pltpu.VMEM)],
        out_specs=pl.BlockSpec(memory_space=pltpu.VMEM),
        out_shape=jax.ShapeDtypeStruct((rows, width), bf),
        scratch_shapes=[
            pltpu.VMEM((4, half, width), bf), pltpu.VMEM((4, half, width), bf), pltpu.VMEM((3, half, width), bf),
            pltpu.VMEM((half, width), bf), pltpu.VMEM((3, half // 4, width), bf), pltpu.VMEM((half // 4, width), bf),
            dma((4,)), dma((4,)), dma((3,)), dma((3,)), dma((3,)), dma((3,)), dma((3,)), dma((3,)), dma((3,)),
        ],
        compiler_params=pltpu.CompilerParams(
            collective_id=collective, has_side_effects=True, vmem_limit_bytes=VMEM_LIMIT
        ),
    )(terms)


def tables(positions):
    half = HEAD_DIM // 2
    frequency = rope_base ** (-2.0 * jnp.arange(half, dtype=jnp.float32) / HEAD_DIM)
    angles = positions.astype(jnp.float32).reshape(-1, 1) * frequency
    cosine, sine = jnp.cos(angles), jnp.sin(angles)
    return (
        jnp.concatenate([cosine] * 4, -1),
        jnp.concatenate([-sine, sine, -sine, sine], -1),
    )


def body(
    hidden_in, cotangent, w_qkv, w_out, w_in, w_mix, attn_gain, mlp_gain, segment_ids, positions
):
    seqs, local, width = hidden_in.shape
    rows = seqs * local
    length = local * lax.axis_size("ctx")
    total = seqs * length
    pairs = HEADS // 2
    bf, f32 = jnp.bfloat16, jnp.float32
    place = lax.axis_index("ctx") * local

    dp_size, ctx_size = lax.axis_size("dp"), lax.axis_size("ctx")
    shard = width // dp_size
    own_gains = jnp.pad(jnp.stack([attn_gain, mlp_gain]), ((0, 30), (0, 256 - shard)))
    own_marks = jnp.pad(jnp.concatenate([segment_ids, positions]), ((0, 8 - 2 * seqs), (0, 0)))
    full_qkv, full_out, full_in, full_mix, gains, hidden_all, marks = gather(
        [w_qkv, w_out, w_in, w_mix, own_gains], [hidden_in, own_marks.reshape(1, 8, local)], 0
    )
    gains = gains.reshape(dp_size, 32, 256)[:, :2, :shard]
    gains = jnp.transpose(gains, (1, 0, 2)).reshape(2, width)
    marks = marks.reshape(ctx_size, 8, local)[:, : 2 * seqs].reshape(ctx_size, 2, seqs, local)
    marks = jnp.transpose(marks, (1, 2, 0, 3)).reshape(2, seqs, length)
    gain_attn, gain_mlp = gains[0].astype(f32), gains[1].astype(f32)

    cos_all, sin_all = tables(marks[1])
    cos_own, sin_own = tables(positions)
    seg_row = marks[0]
    seg_col = jnp.broadcast_to(segment_ids.reshape(rows, 1), (rows, 128))

    inputs = hidden_in.astype(f32).reshape(rows, width)
    normed_attn, attn_norm_back = jax.vjp(norm_gain, inputs, gain_attn)
    x_own = normed_attn.astype(bf)
    x_all = norm_gain(hidden_all.astype(f32).reshape(total, width), gain_attn).astype(bf)

    def const(*shape):
        return pl.BlockSpec(shape, lambda pair: (0,) * len(shape))

    def column(height, offset=0):
        return pl.BlockSpec((height, PAIR), lambda pair: (0, pair + offset))

    shared = [
        const(total, width), const(rows, width),
        column(width), column(width, pairs), column(width, 2 * pairs),
        const(total, PAIR), const(total, PAIR), const(rows, PAIR), const(rows, PAIR),
        const(rows, 128), const(seqs, length),
    ]
    shared_args = (
        x_all, x_own, full_qkv, full_qkv, full_qkv, cos_all, sin_all, cos_own, sin_own, seg_col, seg_row
    )
    params = pltpu.CompilerParams(vmem_limit_bytes=VMEM_LIMIT)
    score_flops = 2 * rows * length * PAIR * HEADS
    q_own, k_all, v_all, attention, logs = pl.pallas_call(
        lambda *refs: forward_kernel(seqs, *refs),
        grid=(pairs,),
        in_specs=shared,
        out_specs=[column(rows), column(total), column(total), column(rows), column(rows)],
        out_shape=[
            jax.ShapeDtypeStruct((rows, width), bf),
            jax.ShapeDtypeStruct((total, width), bf),
            jax.ShapeDtypeStruct((total, width), bf),
            jax.ShapeDtypeStruct((rows, width), f32),
            jax.ShapeDtypeStruct((rows, width), f32),
        ],
        compiler_params=params,
        cost_estimate=pl.CostEstimate(
            flops=2 * score_flops + 4 * total * width * width,
            bytes_accessed=20 * 1024 * 1024, transcendentals=rows * length * HEADS,
        ),
    )(*shared_args)

    attn_low = attention.astype(bf)
    residual = inputs + dot_nn(attn_low, full_out)
    normed_mlp, mlp_norm_back = jax.vjp(norm_gain, residual, gain_mlp)
    mlp_low = normed_mlp.astype(bf)
    wide_proj = dot_nn(mlp_low, full_in)
    activated, geglu_back = jax.vjp(geglu, wide_proj)
    act_low = activated.astype(bf)
    output = residual + dot_nn(act_low, full_mix)
    grad_out = cotangent.reshape(rows, width)
    grad_mix = inner(act_low, grad_out).astype(bf)
    grad_wide = geglu_back(times_back(grad_out, full_mix))[0].astype(bf)
    grad_in = inner(mlp_low, grad_wide).astype(bf)
    grad_norm_in, grad_gain_mlp = mlp_norm_back(times_back(grad_wide, full_in))
    grad_resid = grad_out.astype(f32) + grad_norm_in
    grad_branch = grad_resid.astype(bf)
    grad_attn_out = inner(attn_low, grad_branch).astype(bf)
    g_own = times_back(grad_branch, full_out).astype(bf)

    feature = lax.broadcasted_iota(jnp.int32, (width, HEADS), 0)
    head = lax.broadcasted_iota(jnp.int32, (width, HEADS), 1)
    members = (feature // HEAD_DIM == head).astype(f32)
    opening = (feature == head * HEAD_DIM).astype(f32)
    highest = lax.Precision.HIGHEST
    stats = jnp.concatenate(
        [
            jnp.dot(logs, opening, precision=highest),
            jnp.dot(g_own.astype(f32) * attention, members, precision=highest),
        ],
        -1,
    )
    upper = lax.reduce_precision(stats, 8, 7)
    middle = lax.reduce_precision(stats - upper, 8, 7)
    lower = stats - upper - middle
    packed = jnp.concatenate(
        [g_own, upper.astype(bf), middle.astype(bf), lower.astype(bf), jnp.zeros((rows, 128 - 6 * HEADS), bf)], -1
    )
    (arrived,) = gather([], [packed.reshape(seqs, local, width + 128)], 1)
    pieces = arrived[..., width : width + 6 * HEADS].astype(f32)
    pieces = pieces[..., : 2 * HEADS] + pieces[..., 2 * HEADS : 4 * HEADS] + pieces[..., 4 * HEADS :]
    rows_view = jnp.transpose(pieces.reshape(seqs, length, 2, pairs, 2), (2, 3, 0, 4, 1)).reshape(
        2, pairs, 2 * seqs, length
    )
    k_own = lax.dynamic_slice(k_all.reshape(seqs, length, width), (0, place, 0), (seqs, local, width))
    v_own = lax.dynamic_slice(v_all.reshape(seqs, length, width), (0, place, 0), (seqs, local, width))
    stat_spec = pl.BlockSpec((1, 2 * seqs, length), lambda pair: (pair, 0, 0))
    dw_qkv, back = pl.pallas_call(
        lambda *refs: backward_kernel(seqs, *refs),
        grid=(pairs,),
        in_specs=shared
        + [column(rows)] * 3
        + [column(total)] * 2
        + [column(rows), column(total), column(rows), column(rows), stat_spec, stat_spec],
        out_specs=[
            pl.BlockSpec((3, width, PAIR), lambda pair: (0, 0, pair)),
            const(rows, width),
        ],
        out_shape=[
            jax.ShapeDtypeStruct((3, width, width), bf),
            jax.ShapeDtypeStruct((rows, width), f32),
        ],
        scratch_shapes=[pltpu.VMEM((total, PAIR), bf), pltpu.VMEM((3, rows, PAIR), bf)],
        compiler_params=params,
        cost_estimate=pl.CostEstimate(
            flops=7 * score_flops + 2 * total * width * width + 12 * rows * width * width,
            bytes_accessed=25 * 1024 * 1024, transcendentals=2 * rows * length * HEADS,
        ),
    )(
        *shared_args, q_own, k_own.reshape(rows, width), v_own.reshape(rows, width), k_all, v_all,
        g_own, arrived.reshape(total, width + 128), attention, logs, rows_view[0], rows_view[1],
    )
    grad_norm_attn, grad_gain_attn = attn_norm_back(back)
    grad_hidden = (grad_resid + grad_norm_attn).astype(bf).reshape(hidden_in.shape)

    def by_owner(term):
        return term.reshape(dp_size, -1, width)

    def thirds(term):
        parts = [by_owner(term[..., part * width : (part + 1) * width]) for part in range(3)]
        return parts

    gain_rows = jnp.stack([grad_gain_attn, grad_gain_mlp]).reshape(2, dp_size, shard)
    gain_rows = jnp.pad(jnp.transpose(gain_rows, (1, 0, 2)), ((0, 0), (0, 0), (0, width - shard)))
    stacked = [by_owner(dw_qkv[part]) for part in range(3)] + thirds(grad_in)
    stacked += [by_owner(grad_attn_out), by_owner(grad_mix)]
    used = sum(term.shape[1] for term in stacked)
    padded = -(-(used + 2) // 128) * 128
    stacked.append(jnp.pad(gain_rows.astype(bf), ((0, 0), (0, padded - used - 2), (0, 0))))
    summed = reduce_terms(jnp.concatenate(stacked, 1), 2).astype(f32)
    cuts = [summed[part * shard : (part + 1) * shard] for part in range(7)]
    return (
        output.astype(bf).reshape(hidden_in.shape),
        grad_hidden,
        jnp.concatenate(cuts[:3], 1),
        cuts[6],
        jnp.concatenate(cuts[3:6], 1),
        summed[7 * shard : used],
        summed[used, :shard],
        summed[used + 1, :shard],
    )


def layer(hidden_in, *others):
    sizes = (lax.axis_size("dp"), lax.axis_size("ctx"))
    if sizes != (4, 8) or hidden_in.shape[0] * hidden_in.shape[1] * sizes[1] > 4096:
        return long_body(hidden_in, *others)
    return body(hidden_in, *others)


def solution(mesh):
    placed = (
        P("dp", "ctx", None),
        P("dp", "ctx", None),
        P("dp", None),
        P("dp", None),
        P("dp", None),
        P("dp", None),
        P("dp"),
        P("dp"),
        P("dp", "ctx"),
        P("dp", "ctx"),
    )
    return jax.shard_map(
        layer,
        mesh=mesh,
        in_specs=placed,
        out_specs=(
            P("dp", "ctx", None),
            P("dp", "ctx", None),
            P("dp", None),
            P("dp", None),
            P("dp", None),
            P("dp", None),
            P("dp"),
            P("dp"),
        ),
        check_vma=False,
    )
```

```python
import jax
import jax.numpy as jnp
from jax import lax
from jax.experimental import pallas as pl
from jax.experimental.pallas import tpu as pltpu
from jax.sharding import PartitionSpec as P

HEADS = 12
HEAD_DIM = 64


epsilon = 1e-05
rope_base = 160000.0
masked_score = -1e30


def norm_gain(values, gain_row):
    row_mean = jnp.mean(values, -1, keepdims=True)
    centred = values - row_mean
    return centred * lax.rsqrt(jnp.mean(centred * centred, -1, keepdims=True) + epsilon) * gain_row


def rotate(values, positions, direction):
    half_width = values.shape[-1] // 2
    frequency = rope_base ** (-2.0 * jnp.arange(half_width, dtype=jnp.float32) / values.shape[-1])
    angles = positions.astype(jnp.float32)[..., None] * frequency
    cosine = jnp.cos(angles)[..., None, :]
    sine_part = direction * jnp.sin(angles)[..., None, :]
    first_half = values[..., :half_width]
    second = values[..., half_width:]
    return jnp.concatenate(
        [first_half * cosine - second * sine_part, second * cosine + first_half * sine_part], -1
    )


def geglu(projected):
    half_width = projected.shape[-1] // 2
    return jax.nn.gelu(projected[..., :half_width], approximate=False) * projected[..., half_width:]


def inner(left_arg, right_arg):
    return lax.dot_general(
        left_arg, right_arg, (((0,), (0,)), ((), ())), preferred_element_type=jnp.float32
    )


def times_back(left_arg, right_arg):
    return lax.dot_general(
        left_arg, right_arg, (((1,), (1,)), ((), ())), preferred_element_type=jnp.float32
    )


def heads_view(values):
    return values.reshape(values.shape[:2] + (HEADS, HEAD_DIM))


def same_doc(query_docs, key_docs):
    return query_docs[:, None, :, None] == key_docs[:, None, None, :]


def blockwise(stepper, initial, arrays, block_len):
    key_count = arrays[0].shape[1]
    block_count = key_count // block_len
    pieces = tuple(
        (
            jnp.moveaxis(
                member.reshape(member.shape[:1] + (block_count, block_len) + member.shape[2:]), 1, 0
            )
            for member in arrays
        )
    )
    return lax.scan(lambda running, members: (stepper(running, members), None), initial, pieces)[0]


def long_body(
    hidden_in, cotangent, w_qkv, w_out, w_in, w_mix, attn_gain, mlp_gain, segment_ids, positions
):
    seq_count, local_len, model_width = hidden_in.shape
    row_count = seq_count * local_len
    score_scale = HEAD_DIM ** (-0.5)
    full_qkv, full_out, full_in, full_mix, gain_attn, gain_mlp = (
        lax.all_gather(w_qkv, "dp", axis=0, tiled=True),
        lax.all_gather(w_out, "dp", axis=0, tiled=True),
        lax.all_gather(w_in, "dp", axis=0, tiled=True),
        lax.all_gather(w_mix, "dp", axis=0, tiled=True),
        lax.all_gather(attn_gain, "dp", axis=0, tiled=True),
        lax.all_gather(mlp_gain, "dp", axis=0, tiled=True),
    )
    all_segments = lax.all_gather(segment_ids, "ctx", axis=1, tiled=True)
    inputs = hidden_in.astype(jnp.float32).reshape(row_count, model_width)
    normed_attn, attn_norm_back = jax.vjp(norm_gain, inputs, gain_attn.astype(jnp.float32))
    normed_low = normed_attn.astype(jnp.bfloat16)
    projected = jnp.dot(normed_low, full_qkv, preferred_element_type=jnp.float32).reshape(
        seq_count, local_len, 3, HEADS, HEAD_DIM
    )
    query_heads = rotate(projected[:, :, 0], positions, 1.0).astype(jnp.bfloat16)
    key_low = (
        rotate(projected[:, :, 1], positions, 1.0)
        .astype(jnp.bfloat16)
        .reshape(seq_count, local_len, model_width)
    )
    value_low = projected[:, :, 2].astype(jnp.bfloat16).reshape(seq_count, local_len, model_width)
    key_heads = heads_view(key_low)
    value_heads = heads_view(value_low)

    def attend_block(running, members):
        row_max, row_total, weighted = running
        key_part, value_part, key_docs = members
        scores = (
            jnp.einsum(
                "sqhd,skhd->shqk",
                query_heads,
                heads_view(key_part),
                preferred_element_type=jnp.float32,
            )
            * score_scale
        )
        allowed = same_doc(segment_ids, key_docs)
        newest = jnp.maximum(row_max, jnp.max(jnp.where(allowed, scores, masked_score), -1))
        weights = jnp.where(allowed, jnp.exp(scores - newest[..., None]), 0.0)
        factor = jnp.exp(row_max - newest)
        update = jnp.einsum(
            "shqk,skhd->sqhd",
            weights.astype(jnp.bfloat16),
            heads_view(value_part),
            preferred_element_type=jnp.float32,
        )
        return (
            newest,
            row_total * factor + jnp.sum(weights, -1),
            weighted * jnp.moveaxis(factor, 1, 2)[..., None] + update,
        )

    stat_shape = (seq_count, HEADS, local_len)
    head_shape = (seq_count, local_len, HEADS, HEAD_DIM)
    start_state = (
        jnp.full(stat_shape, masked_score, jnp.float32),
        jnp.zeros(stat_shape, jnp.float32),
        jnp.zeros(head_shape, jnp.float32),
    )
    arriving = (
        lax.all_gather(key_low, "ctx", axis=1, tiled=True),
        lax.all_gather(value_low, "ctx", axis=1, tiled=True),
    )
    key_docs = all_segments
    row_max, row_total, weighted = blockwise(
        attend_block, start_state, (arriving[0], arriving[1], key_docs), local_len
    )
    attention = (weighted / jnp.moveaxis(row_total, 1, 2)[..., None]).reshape(
        row_count, model_width
    )
    log_total = jnp.moveaxis(row_max + jnp.log(row_total), 1, 2)
    attn_low = attention.astype(jnp.bfloat16)
    residual = inputs + jnp.dot(attn_low, full_out, preferred_element_type=jnp.float32)
    normed_mlp, mlp_norm_back = jax.vjp(norm_gain, residual, gain_mlp.astype(jnp.float32))
    mlp_low = normed_mlp.astype(jnp.bfloat16)
    wide_proj = jnp.dot(mlp_low, full_in, preferred_element_type=jnp.float32)
    activated, geglu_back = jax.vjp(geglu, wide_proj)
    act_low = activated.astype(jnp.bfloat16)
    output = residual + jnp.dot(act_low, full_mix, preferred_element_type=jnp.float32)
    grad_out = cotangent.reshape(row_count, model_width)
    grad_mix = inner(act_low, grad_out)
    grad_wide = geglu_back(times_back(grad_out, full_mix))[0].astype(jnp.bfloat16)
    grad_in = inner(mlp_low, grad_wide)
    grad_norm_in, grad_gain_mlp = mlp_norm_back(times_back(grad_wide, full_in))
    grad_resid = grad_out.astype(jnp.float32) + grad_norm_in
    grad_branch = grad_resid.astype(jnp.bfloat16)
    grad_attn_out = inner(attn_low, grad_branch)
    grad_heads = times_back(grad_branch, full_out).astype(jnp.bfloat16)
    grad_view = grad_heads.reshape(head_shape)
    offsets = jnp.sum(grad_view.astype(jnp.float32) * attention.reshape(head_shape), -1)
    all_logs, all_offsets = (
        lax.all_gather(log_total, "ctx", axis=1, tiled=True),
        lax.all_gather(offsets, "ctx", axis=1, tiled=True),
    )
    own_logs = jnp.moveaxis(log_total, 2, 1)[..., None]
    own_offsets = jnp.moveaxis(offsets, 2, 1)[..., None]
    grad_rows = grad_heads.reshape(seq_count, local_len, model_width)
    query_low = query_heads.reshape(seq_count, local_len, model_width)

    def query_terms(key_part, value_part, key_docs):
        scores = (
            jnp.einsum(
                "sqhd,skhd->shqk",
                query_heads,
                heads_view(key_part),
                preferred_element_type=jnp.float32,
            )
            * score_scale
        )
        allowed = same_doc(segment_ids, key_docs)
        attn_probs = jnp.where(allowed, jnp.exp(scores - own_logs), 0.0)
        grad_probs = jnp.einsum(
            "sqhd,skhd->shqk", grad_view, heads_view(value_part), preferred_element_type=jnp.float32
        )
        grad_scores = (attn_probs * (grad_probs - own_offsets)).astype(jnp.bfloat16)
        return (
            jnp.einsum(
                "shqk,skhd->sqhd",
                grad_scores,
                heads_view(key_part),
                preferred_element_type=jnp.float32,
            )
            * score_scale
        )

    def key_terms(query_part, grad_part, query_docs, logs_part, offsets_part):
        query_view = heads_view(query_part)
        grad_part_view = heads_view(grad_part)
        scores = (
            jnp.einsum("sqhd,skhd->shqk", query_view, key_heads, preferred_element_type=jnp.float32)
            * score_scale
        )
        allowed = same_doc(query_docs, segment_ids)
        attn_probs = jnp.where(
            allowed, jnp.exp(scores - jnp.moveaxis(logs_part, 2, 1)[..., None]), 0.0
        )
        grad_value = jnp.einsum(
            "shqk,sqhd->skhd",
            attn_probs.astype(jnp.bfloat16),
            grad_part_view,
            preferred_element_type=jnp.float32,
        )
        grad_probs = jnp.einsum(
            "sqhd,skhd->shqk", grad_part_view, value_heads, preferred_element_type=jnp.float32
        )
        grad_scores = (
            attn_probs * (grad_probs - jnp.moveaxis(offsets_part, 2, 1)[..., None])
        ).astype(jnp.bfloat16)
        grad_key = (
            jnp.einsum(
                "shqk,sqhd->skhd", grad_scores, query_view, preferred_element_type=jnp.float32
            )
            * score_scale
        )
        return (grad_key, grad_value)

    zero_heads = jnp.zeros(head_shape, jnp.float32)

    def query_block(running, members):
        return running + query_terms(members[0], members[1], members[2])

    arriving = (
        lax.all_gather(key_low, "ctx", axis=1, tiled=True),
        lax.all_gather(value_low, "ctx", axis=1, tiled=True),
    )
    grad_query = blockwise(
        query_block, zero_heads, (arriving[0], arriving[1], all_segments), local_len
    )

    def key_block(running, members):
        grad_key, grad_value = key_terms(members[0], members[1], members[2], members[3], members[4])
        return (running[0] + grad_key, running[1] + grad_value)

    grad_key, grad_value = blockwise(
        key_block,
        (zero_heads, zero_heads),
        (
            lax.all_gather(query_low, "ctx", axis=1, tiled=True),
            lax.all_gather(grad_rows, "ctx", axis=1, tiled=True),
        )
        + (all_segments, all_logs, all_offsets),
        local_len,
    )
    grad_qkv = (
        jnp.stack(
            [rotate(grad_query, positions, -1.0), rotate(grad_key, positions, -1.0), grad_value], 2
        )
        .reshape(row_count, 3 * model_width)
        .astype(jnp.bfloat16)
    )
    grad_qkv_w = inner(normed_low, grad_qkv)
    grad_norm_attn, grad_gain_attn = attn_norm_back(times_back(grad_qkv, full_qkv))
    grad_hidden = (grad_resid + grad_norm_attn).astype(jnp.bfloat16).reshape(hidden_in.shape)
    grad_terms = (grad_qkv_w, grad_attn_out, grad_in, grad_mix, grad_gain_attn, grad_gain_mlp)
    summed = (
        lax.psum(grad_terms[0].astype(jnp.bfloat16), "ctx").astype(jnp.float32),
        lax.psum(grad_terms[1].astype(jnp.bfloat16), "ctx").astype(jnp.float32),
        lax.psum(grad_terms[2].astype(jnp.bfloat16), "ctx").astype(jnp.float32),
        lax.psum(grad_terms[3].astype(jnp.bfloat16), "ctx").astype(jnp.float32),
        lax.psum(grad_terms[4].astype(jnp.bfloat16), "ctx").astype(jnp.float32),
        lax.psum(grad_terms[5].astype(jnp.bfloat16), "ctx").astype(jnp.float32),
    )
    owner_grads = (
        lax.psum_scatter(
            summed[0].astype(jnp.bfloat16), "dp", scatter_dimension=0, tiled=True
        ).astype(jnp.float32),
        lax.psum_scatter(
            summed[1].astype(jnp.bfloat16), "dp", scatter_dimension=0, tiled=True
        ).astype(jnp.float32),
        lax.psum_scatter(
            summed[2].astype(jnp.bfloat16), "dp", scatter_dimension=0, tiled=True
        ).astype(jnp.float32),
        lax.psum_scatter(
            summed[3].astype(jnp.bfloat16), "dp", scatter_dimension=0, tiled=True
        ).astype(jnp.float32),
        lax.psum_scatter(
            summed[4].astype(jnp.bfloat16), "dp", scatter_dimension=0, tiled=True
        ).astype(jnp.float32),
        lax.psum_scatter(
            summed[5].astype(jnp.bfloat16), "dp", scatter_dimension=0, tiled=True
        ).astype(jnp.float32),
    )
    return (
        output.astype(jnp.bfloat16).reshape(hidden_in.shape),
        grad_hidden,
        owner_grads[0],
        owner_grads[1],
        owner_grads[2],
        owner_grads[3],
        owner_grads[4],
        owner_grads[5],
    )

PAIR = 2 * HEAD_DIM
VMEM_LIMIT = 56 * 1024 * 1024


def dot_nn(left, right):
    return jnp.dot(left, right, preferred_element_type=jnp.float32)


def turn(values, cosine, sine):
    lane = lax.broadcasted_iota(jnp.int32, values.shape, 1)
    half = HEAD_DIM // 2
    partner = jnp.where(
        lane % HEAD_DIM < half,
        pltpu.roll(values, PAIR - half, 1),
        pltpu.roll(values, half, 1),
    )
    return values * cosine + partner * sine


def head_lanes(shape, head):
    lane = lax.broadcasted_iota(jnp.int32, shape, 1)
    return lane // HEAD_DIM == head


def forward_kernel(
    seqs, x_all, x_own, wq, wk, wv, cos_all, sin_all, cos_own, sin_own, seg_col, seg_row,
    q_out, k_out, v_out, attn_out, log_out,
):
    scale = HEAD_DIM ** (-0.5)
    q_out[...] = turn(dot_nn(x_own[...], wq[...]), cos_own[...], sin_own[...]).astype(jnp.bfloat16)
    k_out[...] = turn(dot_nn(x_all[...], wk[...]), cos_all[...], sin_all[...]).astype(jnp.bfloat16)
    v_out[...] = dot_nn(x_all[...], wv[...]).astype(jnp.bfloat16)
    local = x_own.shape[0] // seqs
    length = x_all.shape[0] // seqs
    for seq in range(seqs):
        own = pl.ds(seq * local, local)
        whole = pl.ds(seq * length, length)
        allowed = seg_col[own, 0:1] == seg_row[seq : seq + 1, :]
        query, key, value = q_out[own, :], k_out[whole, :], v_out[whole, :]
        first = head_lanes(query.shape, 0)
        parts, logs = [], []
        for head in range(2):
            picked = jnp.where(head_lanes(query.shape, head), query * scale, 0).astype(jnp.bfloat16)
            scores = jnp.where(allowed, times_back(picked, key), masked_score)
            top = jnp.max(scores, -1, keepdims=True)
            weights = jnp.exp(scores - top)
            total = jnp.sum(weights, -1, keepdims=True)
            parts.append(dot_nn(weights.astype(jnp.bfloat16), value) / total)
            logs.append(top + jnp.log(total))
        attn_out[own, :] = jnp.where(first, parts[0], parts[1])
        log_out[own, :] = jnp.where(first, logs[0], logs[1])


def backward_kernel(
    seqs, x_all, x_own, wq, wk, wv, cos_all, sin_all, cos_own, sin_own, seg_col, seg_row,
    q_own, k_own, v_own, k_all, v_all, g_own, g_all, attn, logs, log_row, off_row,
    dw_out, r_out, q_all, gp,
):
    scale = HEAD_DIM ** (-0.5)
    q_all[...] = turn(dot_nn(x_all[...], wq[...]), cos_all[...], sin_all[...]).astype(jnp.bfloat16)
    local = x_own.shape[0] // seqs
    length = x_all.shape[0] // seqs
    for seq in range(seqs):
        own = pl.ds(seq * local, local)
        whole = pl.ds(seq * length, length)
        allowed = seg_col[own, 0:1] == seg_row[seq : seq + 1, :]
        query, key, value, grad = q_own[own, :], k_own[own, :], v_own[own, :], g_own[own, :]
        query_w, key_w, value_w, grad_w = q_all[whole, :], k_all[whole, :], v_all[whole, :], g_all[whole, :]
        first = head_lanes(query.shape, 0)
        weighted = grad.astype(jnp.float32) * attn[own, :]
        dq, dk, dv = [], [], []
        for head in range(2):
            mine = head_lanes(query.shape, head)
            offset = jnp.sum(jnp.where(mine, weighted, 0.0), -1, keepdims=True)
            log = logs[own, head * HEAD_DIM : head * HEAD_DIM + 1]
            picked = jnp.where(mine, query * scale, 0).astype(jnp.bfloat16)
            scores = times_back(picked, key_w)
            probs = jnp.exp(jnp.where(allowed, scores - log, masked_score))
            g_probs = times_back(jnp.where(mine, grad, 0).astype(jnp.bfloat16), value_w)
            g_scores = (probs * (g_probs - offset)).astype(jnp.bfloat16)
            dq.append(dot_nn(g_scores, key_w))
            row = 2 * seq + head
            picked = jnp.where(mine, key * scale, 0).astype(jnp.bfloat16)
            scores = times_back(picked, query_w)
            probs = jnp.exp(jnp.where(allowed, scores - log_row[0, row : row + 1, :], masked_score))
            dv.append(dot_nn(probs.astype(jnp.bfloat16), grad_w))
            g_probs = times_back(jnp.where(mine, value, 0).astype(jnp.bfloat16), grad_w)
            g_scores = (probs * (g_probs - off_row[0, row : row + 1, :])).astype(jnp.bfloat16)
            dk.append(dot_nn(g_scores, query_w))
        cosine, sine = cos_own[own, :], -sin_own[own, :]
        gp[0, own, :] = turn(jnp.where(first, dq[0], dq[1]) * scale, cosine, sine).astype(jnp.bfloat16)
        gp[1, own, :] = turn(jnp.where(first, dk[0], dk[1]) * scale, cosine, sine).astype(jnp.bfloat16)
        gp[2, own, :] = jnp.where(first, dv[0], dv[1]).astype(jnp.bfloat16)
    for part in range(3):
        dw_out[part] = inner(x_own[...], gp[part]).astype(jnp.bfloat16)
    back = times_back(gp[0], wq[...]) + times_back(gp[1], wk[...]) + times_back(gp[2], wv[...])

    @pl.when(pl.program_id(0) == 0)
    def _():
        r_out[...] = back

    @pl.when(pl.program_id(0) > 0)
    def _():
        r_out[...] += back


MESH = pl.DeviceIdType.MESH


def partner_of(index, step):
    low = (index % 2 + step % 2) % 2
    high = (index // 2 + step // 2) % 2
    return high * 2 + low


def meet(peers):
    barrier = pltpu.get_barrier_semaphore()
    for peer in peers:
        pl.semaphore_signal(barrier, inc=1, device_id=peer, device_id_type=MESH)
    pl.semaphore_wait(barrier, len(peers))


def neighbours():
    dp, ctx = lax.axis_index("dp"), lax.axis_index("ctx")
    chip, core = ctx // 2, ctx % 2
    across = [(partner_of(dp, step), ctx) for step in (1, 2, 3)]
    along = [(dp, partner_of(chip, step) * 2 + core) for step in (1, 2, 3)]
    return dp, ctx, across, along, (dp, chip * 2 + 1 - core)


def gather_kernel(n_dp, n_ctx, *refs):
    count = n_dp + n_ctx
    ins, outs = refs[:count], refs[count : 2 * count]
    own_sem, send, recv, pass_send, pass_recv = refs[2 * count :]
    dp, ctx, across, along, sibling = neighbours()
    core = ctx % 2
    meet((across if n_dp else []) + along + [sibling])

    def part(which, place_dp, place_ctx):
        out, block = outs[which], ins[which].shape
        if which < n_dp:
            half = block[0] // 2
            return out.at[pl.ds(place_dp * block[0] + core * half, half)]
        return out.at[:, pl.ds(place_ctx * block[1], block[1])]

    jobs, local = [], []
    for which in range(count):
        rows = ins[which].shape[0]
        peers = across if which < n_dp else along
        if which < n_dp:
            source = ins[which].at[pl.ds(core * (rows // 2), rows // 2)]
            own = outs[which].at[pl.ds(dp * rows, rows)]
        else:
            source, own = ins[which], part(which, dp, ctx)
        keep = pltpu.make_async_copy(ins[which], own, own_sem.at[which])
        keep.start()
        local.append(keep)
        for step in range(3):
            job = pltpu.make_async_remote_copy(
                source, part(which, dp, ctx), send.at[which, step], recv.at[which, step],
                device_id=peers[step], device_id_type=MESH,
            )
            job.start()
            jobs.append((which, step, peers[step], job))
    passed = []
    for which in range(n_dp, count):
        job = pltpu.make_async_remote_copy(
            ins[which], part(which, dp, ctx), pass_send.at[which, 3], pass_recv.at[which, 3],
            device_id=sibling, device_id_type=MESH,
        )
        job.start()
        passed.append(job)
    for which, step, peer, job in jobs:
        job.wait_recv()
        landed = part(which, peer[0], peer[1])
        onward = pltpu.make_async_remote_copy(
            landed, landed, pass_send.at[which, step], pass_recv.at[which, step],
            device_id=sibling, device_id_type=MESH,
        )
        onward.start()
        passed.append(onward)
    for keep in local:
        keep.wait()
    for job in jobs:
        job[3].wait_send()
    for job in passed:
        job.wait()


def gather(dp_arrays, ctx_arrays, collective):
    arrays = tuple(dp_arrays) + tuple(ctx_arrays)
    n_dp, count = len(dp_arrays), len(arrays)
    dp_size, ctx_size = lax.axis_size("dp"), lax.axis_size("ctx")
    shapes = [(a.shape[0] * dp_size,) + a.shape[1:] for a in dp_arrays]
    shapes += [(a.shape[0], a.shape[1] * ctx_size) + a.shape[2:] for a in ctx_arrays]
    dma = pltpu.SemaphoreType.DMA
    return pl.pallas_call(
        lambda *refs: gather_kernel(n_dp, count - n_dp, *refs),
        in_specs=[pl.BlockSpec(memory_space=pl.ANY)] * count,
        out_specs=[pl.BlockSpec(memory_space=pl.ANY)] * count,
        out_shape=[jax.ShapeDtypeStruct(shape, a.dtype) for shape, a in zip(shapes, arrays)],
        scratch_shapes=[dma((count,)), dma((count, 3)), dma((count, 3)), dma((count, 4)), dma((count, 4))],
        cost_estimate=pl.CostEstimate(flops=0, bytes_accessed=120 * 1024 * 1024, transcendentals=0),
        compiler_params=pltpu.CompilerParams(collective_id=collective, has_side_effects=True),
    )(*arrays)


def reduce_kernel(
    terms, out, from_core, summed, from_dp, reduced, from_ctx, final,
    core_send, core_recv, dp_send, dp_recv, ctx_send, ctx_recv, spread_send, spread_recv, last,
):
    dp, ctx, across, along, sibling = neighbours()
    chip, core = ctx // 2, ctx % 2
    half, width = reduced.shape
    piece = half // 4
    meet(across + along + [sibling])

    def add(target, sources):
        def chunk(index, carry):
            rows = pl.ds(pl.multiple_of(index * 16, 16), 16)
            value = sources[0][rows, :].astype(jnp.float32)
            for source in sources[1:]:
                value = value + source[rows, :].astype(jnp.float32)
            target[rows, :] = value.astype(jnp.bfloat16)
            return carry

        lax.fori_loop(0, target.shape[0] // 16, chunk, 0)

    swaps = []
    for step in (1, 2, 3, 0):
        owner = partner_of(dp, step)
        swap = pltpu.make_async_remote_copy(
            terms.at[owner, pl.ds((1 - core) * half, half)], from_core.at[step],
            core_send.at[step], core_recv.at[step], device_id=sibling, device_id_type=MESH,
        )
        swap.start()
        swaps.append(swap)
    moves = []
    for step, swap in zip((1, 2, 3, 0), swaps):
        swap.wait_recv()
        owner = partner_of(dp, step)
        add(summed.at[step], [terms.at[owner, pl.ds(core * half, half)], from_core.at[step]])
        if step:
            move = pltpu.make_async_remote_copy(
                summed.at[step], from_dp.at[step - 1], dp_send.at[step - 1], dp_recv.at[step - 1],
                device_id=across[step - 1], device_id_type=MESH,
            )
            move.start()
            moves.append(move)
    for move in moves:
        move.wait_recv()
    add(reduced, [summed.at[0], from_dp.at[0], from_dp.at[1], from_dp.at[2]])
    for step in range(3):
        target = along[step][1] // 2
        move = pltpu.make_async_remote_copy(
            reduced.at[pl.ds(target * piece, piece)], from_ctx.at[step], ctx_send.at[step], ctx_recv.at[step],
            device_id=along[step], device_id_type=MESH,
        )
        move.start()
        moves.append(move)
    for move in moves[3:]:
        move.wait_recv()
    mine = pl.ds(core * half + chip * piece, piece)
    add(final, [reduced.at[pl.ds(chip * piece, piece)], from_ctx.at[0], from_ctx.at[1], from_ctx.at[2]])
    spread = []
    for step in range(3):
        move = pltpu.make_async_remote_copy(
            final, out.at[mine], spread_send.at[step], spread_recv.at[step],
            device_id=along[step], device_id_type=MESH,
        )
        move.start()
        spread.append(move)
    keep = pltpu.make_async_copy(final, out.at[mine], last.at[0])
    keep.start()
    keep.wait()
    for move in spread:
        move.wait_recv()
    whole = pl.ds(core * half, half)
    share = pltpu.make_async_remote_copy(
        out.at[whole], out.at[whole], last.at[1], last.at[2], device_id=sibling, device_id_type=MESH
    )
    share.start()
    for move in swaps + moves + spread:
        move.wait_send()
    share.wait()


def reduce_terms(terms, collective):
    _, rows, width = terms.shape
    half = rows // 2
    bf, dma = jnp.bfloat16, pltpu.SemaphoreType.DMA
    return pl.pallas_call(
        reduce_kernel,
        in_specs=[pl.BlockSpec(memory_space=pltpu.VMEM)],
        out_specs=pl.BlockSpec(memory_space=pltpu.VMEM),
        out_shape=jax.ShapeDtypeStruct((rows, width), bf),
        scratch_shapes=[
            pltpu.VMEM((4, half, width), bf), pltpu.VMEM((4, half, width), bf), pltpu.VMEM((3, half, width), bf),
            pltpu.VMEM((half, width), bf), pltpu.VMEM((3, half // 4, width), bf), pltpu.VMEM((half // 4, width), bf),
            dma((4,)), dma((4,)), dma((3,)), dma((3,)), dma((3,)), dma((3,)), dma((3,)), dma((3,)), dma((3,)),
        ],
        cost_estimate=pl.CostEstimate(flops=0, bytes_accessed=150 * 1024 * 1024, transcendentals=0),
        compiler_params=pltpu.CompilerParams(
            collective_id=collective, has_side_effects=True, vmem_limit_bytes=VMEM_LIMIT
        ),
    )(terms)


def tables(positions):
    half = HEAD_DIM // 2
    frequency = rope_base ** (-2.0 * jnp.arange(half, dtype=jnp.float32) / HEAD_DIM)
    angles = positions.astype(jnp.float32).reshape(-1, 1) * frequency
    cosine, sine = jnp.cos(angles), jnp.sin(angles)
    return (
        jnp.concatenate([cosine] * 4, -1),
        jnp.concatenate([-sine, sine, -sine, sine], -1),
    )


def body(
    hidden_in, cotangent, w_qkv, w_out, w_in, w_mix, attn_gain, mlp_gain, segment_ids, positions
):
    seqs, local, width = hidden_in.shape
    rows = seqs * local
    length = local * lax.axis_size("ctx")
    total = seqs * length
    pairs = HEADS // 2
    bf, f32 = jnp.bfloat16, jnp.float32
    place = lax.axis_index("ctx") * local

    dp_size, ctx_size = lax.axis_size("dp"), lax.axis_size("ctx")
    shard = width // dp_size
    own_gains = jnp.pad(jnp.stack([attn_gain, mlp_gain]), ((0, 30), (0, 256 - shard)))
    own_marks = jnp.pad(jnp.concatenate([segment_ids, positions]), ((0, 8 - 2 * seqs), (0, 0)))
    full_qkv, full_out, full_in, full_mix, gains, hidden_all, marks = gather(
        [w_qkv, w_out, w_in, w_mix, own_gains], [hidden_in, own_marks.reshape(1, 8, local)], 0
    )
    gains = gains.reshape(dp_size, 32, 256)[:, :2, :shard]
    gains = jnp.transpose(gains, (1, 0, 2)).reshape(2, width)
    marks = marks.reshape(ctx_size, 8, local)[:, : 2 * seqs].reshape(ctx_size, 2, seqs, local)
    marks = jnp.transpose(marks, (1, 2, 0, 3)).reshape(2, seqs, length)
    gain_attn, gain_mlp = gains[0].astype(f32), gains[1].astype(f32)

    cos_all, sin_all = tables(marks[1])
    cos_own, sin_own = tables(positions)
    seg_row = marks[0]
    seg_col = jnp.broadcast_to(segment_ids.reshape(rows, 1), (rows, 128))

    inputs = hidden_in.astype(f32).reshape(rows, width)
    normed_attn, attn_norm_back = jax.vjp(norm_gain, inputs, gain_attn)
    x_own = normed_attn.astype(bf)
    x_all = norm_gain(hidden_all.astype(f32).reshape(total, width), gain_attn).astype(bf)

    def const(*shape):
        return pl.BlockSpec(shape, lambda pair: (0,) * len(shape))

    def column(height, offset=0):
        return pl.BlockSpec((height, PAIR), lambda pair: (0, pair + offset))

    shared = [
        const(total, width), const(rows, width),
        column(width), column(width, pairs), column(width, 2 * pairs),
        const(total, PAIR), const(total, PAIR), const(rows, PAIR), const(rows, PAIR),
        const(rows, 128), const(seqs, length),
    ]
    shared_args = (
        x_all, x_own, full_qkv, full_qkv, full_qkv, cos_all, sin_all, cos_own, sin_own, seg_col, seg_row
    )
    params = pltpu.CompilerParams(vmem_limit_bytes=VMEM_LIMIT)
    score_flops = 2 * rows * length * PAIR * HEADS
    q_own, k_all, v_all, attention, logs = pl.pallas_call(
        lambda *refs: forward_kernel(seqs, *refs),
        grid=(pairs,),
        in_specs=shared,
        out_specs=[column(rows), column(total), column(total), column(rows), column(rows)],
        out_shape=[
            jax.ShapeDtypeStruct((rows, width), bf),
            jax.ShapeDtypeStruct((total, width), bf),
            jax.ShapeDtypeStruct((total, width), bf),
            jax.ShapeDtypeStruct((rows, width), f32),
            jax.ShapeDtypeStruct((rows, width), f32),
        ],
        compiler_params=params,
        cost_estimate=pl.CostEstimate(
            flops=2 * score_flops + 4 * total * width * width,
            bytes_accessed=20 * 1024 * 1024, transcendentals=rows * length * HEADS,
        ),
    )(*shared_args)

    attn_low = attention.astype(bf)
    residual = inputs + dot_nn(attn_low, full_out)
    normed_mlp, mlp_norm_back = jax.vjp(norm_gain, residual, gain_mlp)
    mlp_low = normed_mlp.astype(bf)
    wide_proj = dot_nn(mlp_low, full_in)
    activated, geglu_back = jax.vjp(geglu, wide_proj)
    act_low = activated.astype(bf)
    output = residual + dot_nn(act_low, full_mix)
    grad_out = cotangent.reshape(rows, width)
    grad_mix = inner(act_low, grad_out).astype(bf)
    grad_wide = geglu_back(times_back(grad_out, full_mix))[0].astype(bf)
    grad_in = inner(mlp_low, grad_wide).astype(bf)
    grad_norm_in, grad_gain_mlp = mlp_norm_back(times_back(grad_wide, full_in))
    grad_resid = grad_out.astype(f32) + grad_norm_in
    grad_branch = grad_resid.astype(bf)
    grad_attn_out = inner(attn_low, grad_branch).astype(bf)
    g_own = times_back(grad_branch, full_out).astype(bf)

    feature = lax.broadcasted_iota(jnp.int32, (width, HEADS), 0)
    head = lax.broadcasted_iota(jnp.int32, (width, HEADS), 1)
    members = (feature // HEAD_DIM == head).astype(f32)
    opening = (feature == head * HEAD_DIM).astype(f32)
    highest = lax.Precision.HIGHEST
    stats = jnp.concatenate(
        [
            jnp.dot(logs, opening, precision=highest),
            jnp.dot(g_own.astype(f32) * attention, members, precision=highest),
        ],
        -1,
    )
    upper = lax.reduce_precision(stats, 8, 7)
    middle = lax.reduce_precision(stats - upper, 8, 7)
    lower = stats - upper - middle
    packed = jnp.concatenate(
        [g_own, upper.astype(bf), middle.astype(bf), lower.astype(bf), jnp.zeros((rows, 128 - 6 * HEADS), bf)], -1
    )
    (arrived,) = gather([], [packed.reshape(seqs, local, width + 128)], 1)
    pieces = arrived[..., width : width + 6 * HEADS].astype(f32)
    pieces = pieces[..., : 2 * HEADS] + pieces[..., 2 * HEADS : 4 * HEADS] + pieces[..., 4 * HEADS :]
    rows_view = jnp.transpose(pieces.reshape(seqs, length, 2, pairs, 2), (2, 3, 0, 4, 1)).reshape(
        2, pairs, 2 * seqs, length
    )
    k_own = lax.dynamic_slice(k_all.reshape(seqs, length, width), (0, place, 0), (seqs, local, width))
    v_own = lax.dynamic_slice(v_all.reshape(seqs, length, width), (0, place, 0), (seqs, local, width))
    stat_spec = pl.BlockSpec((1, 2 * seqs, length), lambda pair: (pair, 0, 0))
    dw_qkv, back = pl.pallas_call(
        lambda *refs: backward_kernel(seqs, *refs),
        grid=(pairs,),
        in_specs=shared
        + [column(rows)] * 3
        + [column(total)] * 2
        + [column(rows), column(total), column(rows), column(rows), stat_spec, stat_spec],
        out_specs=[
            pl.BlockSpec((3, width, PAIR), lambda pair: (0, 0, pair)),
            const(rows, width),
        ],
        out_shape=[
            jax.ShapeDtypeStruct((3, width, width), bf),
            jax.ShapeDtypeStruct((rows, width), f32),
        ],
        scratch_shapes=[pltpu.VMEM((total, PAIR), bf), pltpu.VMEM((3, rows, PAIR), bf)],
        compiler_params=params,
        cost_estimate=pl.CostEstimate(
            flops=7 * score_flops + 2 * total * width * width + 12 * rows * width * width,
            bytes_accessed=25 * 1024 * 1024, transcendentals=2 * rows * length * HEADS,
        ),
    )(
        *shared_args, q_own, k_own.reshape(rows, width), v_own.reshape(rows, width), k_all, v_all,
        g_own, arrived.reshape(total, width + 128), attention, logs, rows_view[0], rows_view[1],
    )
    grad_norm_attn, grad_gain_attn = attn_norm_back(back)
    grad_hidden = (grad_resid + grad_norm_attn).astype(bf).reshape(hidden_in.shape)

    def by_owner(term):
        return term.reshape(dp_size, -1, width)

    def thirds(term):
        parts = [by_owner(term[..., part * width : (part + 1) * width]) for part in range(3)]
        return parts

    gain_rows = jnp.stack([grad_gain_attn, grad_gain_mlp]).reshape(2, dp_size, shard)
    gain_rows = jnp.pad(jnp.transpose(gain_rows, (1, 0, 2)), ((0, 0), (0, 0), (0, width - shard)))
    early = jnp.concatenate(thirds(grad_in) + [by_owner(grad_attn_out), by_owner(grad_mix)], 1)
    early = lax.psum_scatter(early, "dp", scatter_dimension=0, tiled=True)
    stacked = [by_owner(dw_qkv[part]) for part in range(3)]
    used = 3 * shard
    padded = -(-(used + 2) // 128) * 128
    stacked.append(jnp.pad(gain_rows.astype(bf), ((0, 0), (0, padded - used - 2), (0, 0))))
    early, late = lax.optimization_barrier((early, jnp.concatenate(stacked, 1)))
    early = lax.psum(early, "ctx")[0].astype(f32)
    summed = reduce_terms(late, 2).astype(f32)
    cuts = [early[part * shard : (part + 1) * shard] for part in range(4)]
    return (
        output.astype(bf).reshape(hidden_in.shape),
        grad_hidden,
        jnp.concatenate([summed[part * shard : (part + 1) * shard] for part in range(3)], 1),
        cuts[3],
        jnp.concatenate(cuts[:3], 1),
        early[4 * shard :],
        summed[used, :shard],
        summed[used + 1, :shard],
    )


def layer(hidden_in, *others):
    sizes = (lax.axis_size("dp"), lax.axis_size("ctx"))
    if sizes != (4, 8) or hidden_in.shape[0] * hidden_in.shape[1] * sizes[1] > 4096:
        return long_body(hidden_in, *others)
    return body(hidden_in, *others)


def solution(mesh):
    placed = (
        P("dp", "ctx", None),
        P("dp", "ctx", None),
        P("dp", None),
        P("dp", None),
        P("dp", None),
        P("dp", None),
        P("dp"),
        P("dp"),
        P("dp", "ctx"),
        P("dp", "ctx"),
    )
    return jax.shard_map(
        layer,
        mesh=mesh,
        in_specs=placed,
        out_specs=(
            P("dp", "ctx", None),
            P("dp", "ctx", None),
            P("dp", None),
            P("dp", None),
            P("dp", None),
            P("dp", None),
            P("dp"),
            P("dp"),
        ),
        check_vma=False,
    )
```

```python
import jax
import jax.numpy as jnp
from jax import lax
from jax.experimental import pallas as pl
from jax.experimental.pallas import tpu as pltpu
from jax.sharding import PartitionSpec as P

HEADS = 12
HEAD_DIM = 64


epsilon = 1e-05
rope_base = 160000.0
masked_score = -1e30


def norm_gain(values, gain_row):
    row_mean = jnp.mean(values, -1, keepdims=True)
    centred = values - row_mean
    return centred * lax.rsqrt(jnp.mean(centred * centred, -1, keepdims=True) + epsilon) * gain_row


def rotate(values, positions, direction):
    half_width = values.shape[-1] // 2
    frequency = rope_base ** (-2.0 * jnp.arange(half_width, dtype=jnp.float32) / values.shape[-1])
    angles = positions.astype(jnp.float32)[..., None] * frequency
    cosine = jnp.cos(angles)[..., None, :]
    sine_part = direction * jnp.sin(angles)[..., None, :]
    first_half = values[..., :half_width]
    second = values[..., half_width:]
    return jnp.concatenate(
        [first_half * cosine - second * sine_part, second * cosine + first_half * sine_part], -1
    )


def geglu(projected):
    half_width = projected.shape[-1] // 2
    return jax.nn.gelu(projected[..., :half_width], approximate=False) * projected[..., half_width:]


def inner(left_arg, right_arg):
    return lax.dot_general(
        left_arg, right_arg, (((0,), (0,)), ((), ())), preferred_element_type=jnp.float32
    )


def times_back(left_arg, right_arg):
    return lax.dot_general(
        left_arg, right_arg, (((1,), (1,)), ((), ())), preferred_element_type=jnp.float32
    )


def heads_view(values):
    return values.reshape(values.shape[:2] + (HEADS, HEAD_DIM))


def same_doc(query_docs, key_docs):
    return query_docs[:, None, :, None] == key_docs[:, None, None, :]


def blockwise(stepper, initial, arrays, block_len):
    key_count = arrays[0].shape[1]
    block_count = key_count // block_len
    pieces = tuple(
        (
            jnp.moveaxis(
                member.reshape(member.shape[:1] + (block_count, block_len) + member.shape[2:]), 1, 0
            )
            for member in arrays
        )
    )
    return lax.scan(lambda running, members: (stepper(running, members), None), initial, pieces)[0]


def long_body(
    hidden_in, cotangent, w_qkv, w_out, w_in, w_mix, attn_gain, mlp_gain, segment_ids, positions
):
    seq_count, local_len, model_width = hidden_in.shape
    row_count = seq_count * local_len
    score_scale = HEAD_DIM ** (-0.5)
    full_qkv, full_out, full_in, full_mix, gain_attn, gain_mlp = (
        lax.all_gather(w_qkv, "dp", axis=0, tiled=True),
        lax.all_gather(w_out, "dp", axis=0, tiled=True),
        lax.all_gather(w_in, "dp", axis=0, tiled=True),
        lax.all_gather(w_mix, "dp", axis=0, tiled=True),
        lax.all_gather(attn_gain, "dp", axis=0, tiled=True),
        lax.all_gather(mlp_gain, "dp", axis=0, tiled=True),
    )
    all_segments = lax.all_gather(segment_ids, "ctx", axis=1, tiled=True)
    inputs = hidden_in.astype(jnp.float32).reshape(row_count, model_width)
    normed_attn, attn_norm_back = jax.vjp(norm_gain, inputs, gain_attn.astype(jnp.float32))
    normed_low = normed_attn.astype(jnp.bfloat16)
    projected = jnp.dot(normed_low, full_qkv, preferred_element_type=jnp.float32).reshape(
        seq_count, local_len, 3, HEADS, HEAD_DIM
    )
    query_heads = rotate(projected[:, :, 0], positions, 1.0).astype(jnp.bfloat16)
    key_low = (
        rotate(projected[:, :, 1], positions, 1.0)
        .astype(jnp.bfloat16)
        .reshape(seq_count, local_len, model_width)
    )
    value_low = projected[:, :, 2].astype(jnp.bfloat16).reshape(seq_count, local_len, model_width)
    key_heads = heads_view(key_low)
    value_heads = heads_view(value_low)

    def attend_block(running, members):
        row_max, row_total, weighted = running
        key_part, value_part, key_docs = members
        scores = (
            jnp.einsum(
                "sqhd,skhd->shqk",
                query_heads,
                heads_view(key_part),
                preferred_element_type=jnp.float32,
            )
            * score_scale
        )
        allowed = same_doc(segment_ids, key_docs)
        newest = jnp.maximum(row_max, jnp.max(jnp.where(allowed, scores, masked_score), -1))
        weights = jnp.where(allowed, jnp.exp(scores - newest[..., None]), 0.0)
        factor = jnp.exp(row_max - newest)
        update = jnp.einsum(
            "shqk,skhd->sqhd",
            weights.astype(jnp.bfloat16),
            heads_view(value_part),
            preferred_element_type=jnp.float32,
        )
        return (
            newest,
            row_total * factor + jnp.sum(weights, -1),
            weighted * jnp.moveaxis(factor, 1, 2)[..., None] + update,
        )

    stat_shape = (seq_count, HEADS, local_len)
    head_shape = (seq_count, local_len, HEADS, HEAD_DIM)
    start_state = (
        jnp.full(stat_shape, masked_score, jnp.float32),
        jnp.zeros(stat_shape, jnp.float32),
        jnp.zeros(head_shape, jnp.float32),
    )
    arriving = (
        lax.all_gather(key_low, "ctx", axis=1, tiled=True),
        lax.all_gather(value_low, "ctx", axis=1, tiled=True),
    )
    key_docs = all_segments
    row_max, row_total, weighted = blockwise(
        attend_block, start_state, (arriving[0], arriving[1], key_docs), local_len
    )
    attention = (weighted / jnp.moveaxis(row_total, 1, 2)[..., None]).reshape(
        row_count, model_width
    )
    log_total = jnp.moveaxis(row_max + jnp.log(row_total), 1, 2)
    attn_low = attention.astype(jnp.bfloat16)
    residual = inputs + jnp.dot(attn_low, full_out, preferred_element_type=jnp.float32)
    normed_mlp, mlp_norm_back = jax.vjp(norm_gain, residual, gain_mlp.astype(jnp.float32))
    mlp_low = normed_mlp.astype(jnp.bfloat16)
    wide_proj = jnp.dot(mlp_low, full_in, preferred_element_type=jnp.float32)
    activated, geglu_back = jax.vjp(geglu, wide_proj)
    act_low = activated.astype(jnp.bfloat16)
    output = residual + jnp.dot(act_low, full_mix, preferred_element_type=jnp.float32)
    grad_out = cotangent.reshape(row_count, model_width)
    grad_mix = inner(act_low, grad_out)
    grad_wide = geglu_back(times_back(grad_out, full_mix))[0].astype(jnp.bfloat16)
    grad_in = inner(mlp_low, grad_wide)
    grad_norm_in, grad_gain_mlp = mlp_norm_back(times_back(grad_wide, full_in))
    grad_resid = grad_out.astype(jnp.float32) + grad_norm_in
    grad_branch = grad_resid.astype(jnp.bfloat16)
    grad_attn_out = inner(attn_low, grad_branch)
    grad_heads = times_back(grad_branch, full_out).astype(jnp.bfloat16)
    grad_view = grad_heads.reshape(head_shape)
    offsets = jnp.sum(grad_view.astype(jnp.float32) * attention.reshape(head_shape), -1)
    all_logs, all_offsets = (
        lax.all_gather(log_total, "ctx", axis=1, tiled=True),
        lax.all_gather(offsets, "ctx", axis=1, tiled=True),
    )
    own_logs = jnp.moveaxis(log_total, 2, 1)[..., None]
    own_offsets = jnp.moveaxis(offsets, 2, 1)[..., None]
    grad_rows = grad_heads.reshape(seq_count, local_len, model_width)
    query_low = query_heads.reshape(seq_count, local_len, model_width)

    def query_terms(key_part, value_part, key_docs):
        scores = (
            jnp.einsum(
                "sqhd,skhd->shqk",
                query_heads,
                heads_view(key_part),
                preferred_element_type=jnp.float32,
            )
            * score_scale
        )
        allowed = same_doc(segment_ids, key_docs)
        attn_probs = jnp.where(allowed, jnp.exp(scores - own_logs), 0.0)
        grad_probs = jnp.einsum(
            "sqhd,skhd->shqk", grad_view, heads_view(value_part), preferred_element_type=jnp.float32
        )
        grad_scores = (attn_probs * (grad_probs - own_offsets)).astype(jnp.bfloat16)
        return (
            jnp.einsum(
                "shqk,skhd->sqhd",
                grad_scores,
                heads_view(key_part),
                preferred_element_type=jnp.float32,
            )
            * score_scale
        )

    def key_terms(query_part, grad_part, query_docs, logs_part, offsets_part):
        query_view = heads_view(query_part)
        grad_part_view = heads_view(grad_part)
        scores = (
            jnp.einsum("sqhd,skhd->shqk", query_view, key_heads, preferred_element_type=jnp.float32)
            * score_scale
        )
        allowed = same_doc(query_docs, segment_ids)
        attn_probs = jnp.where(
            allowed, jnp.exp(scores - jnp.moveaxis(logs_part, 2, 1)[..., None]), 0.0
        )
        grad_value = jnp.einsum(
            "shqk,sqhd->skhd",
            attn_probs.astype(jnp.bfloat16),
            grad_part_view,
            preferred_element_type=jnp.float32,
        )
        grad_probs = jnp.einsum(
            "sqhd,skhd->shqk", grad_part_view, value_heads, preferred_element_type=jnp.float32
        )
        grad_scores = (
            attn_probs * (grad_probs - jnp.moveaxis(offsets_part, 2, 1)[..., None])
        ).astype(jnp.bfloat16)
        grad_key = (
            jnp.einsum(
                "shqk,sqhd->skhd", grad_scores, query_view, preferred_element_type=jnp.float32
            )
            * score_scale
        )
        return (grad_key, grad_value)

    zero_heads = jnp.zeros(head_shape, jnp.float32)

    def query_block(running, members):
        return running + query_terms(members[0], members[1], members[2])

    arriving = (
        lax.all_gather(key_low, "ctx", axis=1, tiled=True),
        lax.all_gather(value_low, "ctx", axis=1, tiled=True),
    )
    grad_query = blockwise(
        query_block, zero_heads, (arriving[0], arriving[1], all_segments), local_len
    )

    def key_block(running, members):
        grad_key, grad_value = key_terms(members[0], members[1], members[2], members[3], members[4])
        return (running[0] + grad_key, running[1] + grad_value)

    grad_key, grad_value = blockwise(
        key_block,
        (zero_heads, zero_heads),
        (
            lax.all_gather(query_low, "ctx", axis=1, tiled=True),
            lax.all_gather(grad_rows, "ctx", axis=1, tiled=True),
        )
        + (all_segments, all_logs, all_offsets),
        local_len,
    )
    grad_qkv = (
        jnp.stack(
            [rotate(grad_query, positions, -1.0), rotate(grad_key, positions, -1.0), grad_value], 2
        )
        .reshape(row_count, 3 * model_width)
        .astype(jnp.bfloat16)
    )
    grad_qkv_w = inner(normed_low, grad_qkv)
    grad_norm_attn, grad_gain_attn = attn_norm_back(times_back(grad_qkv, full_qkv))
    grad_hidden = (grad_resid + grad_norm_attn).astype(jnp.bfloat16).reshape(hidden_in.shape)
    grad_terms = (grad_qkv_w, grad_attn_out, grad_in, grad_mix, grad_gain_attn, grad_gain_mlp)
    summed = (
        lax.psum(grad_terms[0].astype(jnp.bfloat16), "ctx").astype(jnp.float32),
        lax.psum(grad_terms[1].astype(jnp.bfloat16), "ctx").astype(jnp.float32),
        lax.psum(grad_terms[2].astype(jnp.bfloat16), "ctx").astype(jnp.float32),
        lax.psum(grad_terms[3].astype(jnp.bfloat16), "ctx").astype(jnp.float32),
        lax.psum(grad_terms[4].astype(jnp.bfloat16), "ctx").astype(jnp.float32),
        lax.psum(grad_terms[5].astype(jnp.bfloat16), "ctx").astype(jnp.float32),
    )
    owner_grads = (
        lax.psum_scatter(
            summed[0].astype(jnp.bfloat16), "dp", scatter_dimension=0, tiled=True
        ).astype(jnp.float32),
        lax.psum_scatter(
            summed[1].astype(jnp.bfloat16), "dp", scatter_dimension=0, tiled=True
        ).astype(jnp.float32),
        lax.psum_scatter(
            summed[2].astype(jnp.bfloat16), "dp", scatter_dimension=0, tiled=True
        ).astype(jnp.float32),
        lax.psum_scatter(
            summed[3].astype(jnp.bfloat16), "dp", scatter_dimension=0, tiled=True
        ).astype(jnp.float32),
        lax.psum_scatter(
            summed[4].astype(jnp.bfloat16), "dp", scatter_dimension=0, tiled=True
        ).astype(jnp.float32),
        lax.psum_scatter(
            summed[5].astype(jnp.bfloat16), "dp", scatter_dimension=0, tiled=True
        ).astype(jnp.float32),
    )
    return (
        output.astype(jnp.bfloat16).reshape(hidden_in.shape),
        grad_hidden,
        owner_grads[0],
        owner_grads[1],
        owner_grads[2],
        owner_grads[3],
        owner_grads[4],
        owner_grads[5],
    )

PAIR = 2 * HEAD_DIM
VMEM_LIMIT = 56 * 1024 * 1024


def dot_nn(left, right):
    return jnp.dot(left, right, preferred_element_type=jnp.float32)


def turn(values, cosine, sine):
    lane = lax.broadcasted_iota(jnp.int32, values.shape, 1)
    half = HEAD_DIM // 2
    partner = jnp.where(
        lane % HEAD_DIM < half,
        pltpu.roll(values, PAIR - half, 1),
        pltpu.roll(values, half, 1),
    )
    return values * cosine + partner * sine


def head_lanes(shape, head):
    lane = lax.broadcasted_iota(jnp.int32, shape, 1)
    return lane // HEAD_DIM == head


def forward_kernel(
    seqs, x_all, x_own, wq, wk, wv, cos_all, sin_all, cos_own, sin_own, seg_col, seg_row,
    q_out, k_out, v_out, attn_out, log_out,
):
    scale = HEAD_DIM ** (-0.5)
    q_out[...] = turn(dot_nn(x_own[...], wq[...]), cos_own[...], sin_own[...]).astype(jnp.bfloat16)
    k_out[...] = turn(dot_nn(x_all[...], wk[...]), cos_all[...], sin_all[...]).astype(jnp.bfloat16)
    v_out[...] = dot_nn(x_all[...], wv[...]).astype(jnp.bfloat16)
    local = x_own.shape[0] // seqs
    length = x_all.shape[0] // seqs
    for seq in range(seqs):
        own = pl.ds(seq * local, local)
        whole = pl.ds(seq * length, length)
        allowed = seg_col[own, 0:1] == seg_row[seq : seq + 1, :]
        query, key, value = q_out[own, :], k_out[whole, :], v_out[whole, :]
        first = head_lanes(query.shape, 0)
        parts, logs = [], []
        for head in range(2):
            picked = jnp.where(head_lanes(query.shape, head), query * scale, 0).astype(jnp.bfloat16)
            scores = jnp.where(allowed, times_back(picked, key), masked_score)
            top = jnp.max(scores, -1, keepdims=True)
            weights = jnp.exp(scores - top)
            total = jnp.sum(weights, -1, keepdims=True)
            parts.append(dot_nn(weights.astype(jnp.bfloat16), value) / total)
            logs.append(top + jnp.log(total))
        attn_out[own, :] = jnp.where(first, parts[0], parts[1])
        log_out[own, :] = jnp.where(first, logs[0], logs[1])


def backward_kernel(
    seqs, x_all, x_own, wq, wk, wv, cos_all, sin_all, cos_own, sin_own, seg_col, seg_row,
    q_own, k_own, v_own, k_all, v_all, g_own, g_all, attn, logs, log_row, off_row,
    dw_out, r_out, q_all, gp,
):
    scale = HEAD_DIM ** (-0.5)
    q_all[...] = turn(dot_nn(x_all[...], wq[...]), cos_all[...], sin_all[...]).astype(jnp.bfloat16)
    local = x_own.shape[0] // seqs
    length = x_all.shape[0] // seqs
    for seq in range(seqs):
        own = pl.ds(seq * local, local)
        whole = pl.ds(seq * length, length)
        allowed = seg_col[own, 0:1] == seg_row[seq : seq + 1, :]
        query, key, value, grad = q_own[own, :], k_own[own, :], v_own[own, :], g_own[own, :]
        query_w, key_w, value_w, grad_w = q_all[whole, :], k_all[whole, :], v_all[whole, :], g_all[whole, :]
        first = head_lanes(query.shape, 0)
        weighted = grad.astype(jnp.float32) * attn[own, :]
        dq, dk, dv = [], [], []
        for head in range(2):
            mine = head_lanes(query.shape, head)
            offset = jnp.sum(jnp.where(mine, weighted, 0.0), -1, keepdims=True)
            log = logs[own, head * HEAD_DIM : head * HEAD_DIM + 1]
            picked = jnp.where(mine, query * scale, 0).astype(jnp.bfloat16)
            scores = times_back(picked, key_w)
            probs = jnp.exp(jnp.where(allowed, scores - log, masked_score))
            g_probs = times_back(jnp.where(mine, grad, 0).astype(jnp.bfloat16), value_w)
            g_scores = (probs * (g_probs - offset)).astype(jnp.bfloat16)
            dq.append(dot_nn(g_scores, key_w))
            row = 2 * seq + head
            picked = jnp.where(mine, key * scale, 0).astype(jnp.bfloat16)
            scores = times_back(picked, query_w)
            probs = jnp.exp(jnp.where(allowed, scores - log_row[0, row : row + 1, :], masked_score))
            dv.append(dot_nn(probs.astype(jnp.bfloat16), grad_w))
            g_probs = times_back(jnp.where(mine, value, 0).astype(jnp.bfloat16), grad_w)
            g_scores = (probs * (g_probs - off_row[0, row : row + 1, :])).astype(jnp.bfloat16)
            dk.append(dot_nn(g_scores, query_w))
        cosine, sine = cos_own[own, :], -sin_own[own, :]
        gp[0, own, :] = turn(jnp.where(first, dq[0], dq[1]) * scale, cosine, sine).astype(jnp.bfloat16)
        gp[1, own, :] = turn(jnp.where(first, dk[0], dk[1]) * scale, cosine, sine).astype(jnp.bfloat16)
        gp[2, own, :] = jnp.where(first, dv[0], dv[1]).astype(jnp.bfloat16)
    for part in range(3):
        dw_out[part] = inner(x_own[...], gp[part]).astype(jnp.bfloat16)
    back = times_back(gp[0], wq[...]) + times_back(gp[1], wk[...]) + times_back(gp[2], wv[...])

    @pl.when(pl.program_id(0) == 0)
    def _():
        r_out[...] = back

    @pl.when(pl.program_id(0) > 0)
    def _():
        r_out[...] += back


MESH = pl.DeviceIdType.MESH


def partner_of(index, step):
    low = (index % 2 + step % 2) % 2
    high = (index // 2 + step // 2) % 2
    return high * 2 + low


def meet(peers):
    barrier = pltpu.get_barrier_semaphore()
    for peer in peers:
        pl.semaphore_signal(barrier, inc=1, device_id=peer, device_id_type=MESH)
    pl.semaphore_wait(barrier, len(peers))


def neighbours():
    dp, ctx = lax.axis_index("dp"), lax.axis_index("ctx")
    chip, core = ctx // 2, ctx % 2
    across = [(partner_of(dp, step), ctx) for step in (1, 2, 3)]
    along = [(dp, partner_of(chip, step) * 2 + core) for step in (1, 2, 3)]
    return dp, ctx, across, along, (dp, chip * 2 + 1 - core)


def gather_kernel(n_dp, n_ctx, *refs):
    count = n_dp + n_ctx
    ins, outs = refs[:count], refs[count : 2 * count]
    own_sem, send, recv, pass_send, pass_recv = refs[2 * count :]
    dp, ctx, across, along, sibling = neighbours()
    core = ctx % 2
    meet((across if n_dp else []) + along + [sibling])

    def part(which, place_dp, place_ctx):
        out, block = outs[which], ins[which].shape
        if which < n_dp:
            half = block[0] // 2
            return out.at[pl.ds(place_dp * block[0] + core * half, half)]
        return out.at[:, pl.ds(place_ctx * block[1], block[1])]

    jobs, local = [], []
    for which in range(count):
        rows = ins[which].shape[0]
        peers = across if which < n_dp else along
        if which < n_dp:
            source = ins[which].at[pl.ds(core * (rows // 2), rows // 2)]
            own = outs[which].at[pl.ds(dp * rows, rows)]
        else:
            source, own = ins[which], part(which, dp, ctx)
        keep = pltpu.make_async_copy(ins[which], own, own_sem.at[which])
        keep.start()
        local.append(keep)
        for step in range(3):
            job = pltpu.make_async_remote_copy(
                source, part(which, dp, ctx), send.at[which, step], recv.at[which, step],
                device_id=peers[step], device_id_type=MESH,
            )
            job.start()
            jobs.append((which, step, peers[step], job))
    passed = []
    for which in range(n_dp, count):
        job = pltpu.make_async_remote_copy(
            ins[which], part(which, dp, ctx), pass_send.at[which, 3], pass_recv.at[which, 3],
            device_id=sibling, device_id_type=MESH,
        )
        job.start()
        passed.append(job)
    for which, step, peer, job in jobs:
        job.wait_recv()
        landed = part(which, peer[0], peer[1])
        onward = pltpu.make_async_remote_copy(
            landed, landed, pass_send.at[which, step], pass_recv.at[which, step],
            device_id=sibling, device_id_type=MESH,
        )
        onward.start()
        passed.append(onward)
    for keep in local:
        keep.wait()
    for job in jobs:
        job[3].wait_send()
    for job in passed:
        job.wait()


def gather(dp_arrays, ctx_arrays, collective):
    arrays = tuple(dp_arrays) + tuple(ctx_arrays)
    n_dp, count = len(dp_arrays), len(arrays)
    dp_size, ctx_size = lax.axis_size("dp"), lax.axis_size("ctx")
    shapes = [(a.shape[0] * dp_size,) + a.shape[1:] for a in dp_arrays]
    shapes += [(a.shape[0], a.shape[1] * ctx_size) + a.shape[2:] for a in ctx_arrays]
    dma = pltpu.SemaphoreType.DMA
    return pl.pallas_call(
        lambda *refs: gather_kernel(n_dp, count - n_dp, *refs),
        in_specs=[pl.BlockSpec(memory_space=pl.ANY)] * count,
        out_specs=[pl.BlockSpec(memory_space=pl.ANY)] * count,
        out_shape=[jax.ShapeDtypeStruct(shape, a.dtype) for shape, a in zip(shapes, arrays)],
        scratch_shapes=[dma((count,)), dma((count, 3)), dma((count, 3)), dma((count, 4)), dma((count, 4))],
        cost_estimate=pl.CostEstimate(flops=0, bytes_accessed=120 * 1024 * 1024, transcendentals=0),
        compiler_params=pltpu.CompilerParams(collective_id=collective, has_side_effects=True),
    )(*arrays)


def reduce_kernel(
    terms, out, from_core, summed, from_dp, reduced, from_ctx, final,
    core_send, core_recv, dp_send, dp_recv, ctx_send, ctx_recv, spread_send, spread_recv, last,
):
    dp, ctx, across, along, sibling = neighbours()
    chip, core = ctx // 2, ctx % 2
    half, width = reduced.shape
    piece = half // 4
    meet(across + along + [sibling])

    def add(target, sources):
        def chunk(index, carry):
            rows = pl.ds(pl.multiple_of(index * 16, 16), 16)
            value = sources[0][rows, :].astype(jnp.float32)
            for source in sources[1:]:
                value = value + source[rows, :].astype(jnp.float32)
            target[rows, :] = value.astype(jnp.bfloat16)
            return carry

        lax.fori_loop(0, target.shape[0] // 16, chunk, 0)

    swaps = []
    for step in (1, 2, 3, 0):
        owner = partner_of(dp, step)
        swap = pltpu.make_async_remote_copy(
            terms.at[owner, pl.ds((1 - core) * half, half)], from_core.at[step],
            core_send.at[step], core_recv.at[step], device_id=sibling, device_id_type=MESH,
        )
        swap.start()
        swaps.append(swap)
    moves = []
    for step, swap in zip((1, 2, 3, 0), swaps):
        swap.wait_recv()
        owner = partner_of(dp, step)
        add(summed.at[step], [terms.at[owner, pl.ds(core * half, half)], from_core.at[step]])
        if step:
            move = pltpu.make_async_remote_copy(
                summed.at[step], from_dp.at[step - 1], dp_send.at[step - 1], dp_recv.at[step - 1],
                device_id=across[step - 1], device_id_type=MESH,
            )
            move.start()
            moves.append(move)
    for move in moves:
        move.wait_recv()
    add(reduced, [summed.at[0], from_dp.at[0], from_dp.at[1], from_dp.at[2]])
    for step in range(3):
        target = along[step][1] // 2
        move = pltpu.make_async_remote_copy(
            reduced.at[pl.ds(target * piece, piece)], from_ctx.at[step], ctx_send.at[step], ctx_recv.at[step],
            device_id=along[step], device_id_type=MESH,
        )
        move.start()
        moves.append(move)
    for move in moves[3:]:
        move.wait_recv()
    mine = pl.ds(core * half + chip * piece, piece)
    add(final, [reduced.at[pl.ds(chip * piece, piece)], from_ctx.at[0], from_ctx.at[1], from_ctx.at[2]])
    spread = []
    for step in range(3):
        move = pltpu.make_async_remote_copy(
            final, out.at[mine], spread_send.at[step], spread_recv.at[step],
            device_id=along[step], device_id_type=MESH,
        )
        move.start()
        spread.append(move)
    keep = pltpu.make_async_copy(final, out.at[mine], last.at[0])
    keep.start()
    keep.wait()
    for move in spread:
        move.wait_recv()
    whole = pl.ds(core * half, half)
    share = pltpu.make_async_remote_copy(
        out.at[whole], out.at[whole], last.at[1], last.at[2], device_id=sibling, device_id_type=MESH
    )
    share.start()
    for move in swaps + moves + spread:
        move.wait_send()
    share.wait()


def reduce_terms(terms, collective):
    _, rows, width = terms.shape
    half = rows // 2
    bf, dma = jnp.bfloat16, pltpu.SemaphoreType.DMA
    return pl.pallas_call(
        reduce_kernel,
        in_specs=[pl.BlockSpec(memory_space=pltpu.VMEM)],
        out_specs=pl.BlockSpec(memory_space=pltpu.VMEM),
        out_shape=jax.ShapeDtypeStruct((rows, width), bf),
        scratch_shapes=[
            pltpu.VMEM((4, half, width), bf), pltpu.VMEM((4, half, width), bf), pltpu.VMEM((3, half, width), bf),
            pltpu.VMEM((half, width), bf), pltpu.VMEM((3, half // 4, width), bf), pltpu.VMEM((half // 4, width), bf),
            dma((4,)), dma((4,)), dma((3,)), dma((3,)), dma((3,)), dma((3,)), dma((3,)), dma((3,)), dma((3,)),
        ],
        cost_estimate=pl.CostEstimate(flops=0, bytes_accessed=150 * 1024 * 1024, transcendentals=0),
        compiler_params=pltpu.CompilerParams(
            collective_id=collective, has_side_effects=True, vmem_limit_bytes=VMEM_LIMIT
        ),
    )(terms)


def tables(positions):
    half = HEAD_DIM // 2
    frequency = rope_base ** (-2.0 * jnp.arange(half, dtype=jnp.float32) / HEAD_DIM)
    angles = positions.astype(jnp.float32).reshape(-1, 1) * frequency
    cosine, sine = jnp.cos(angles), jnp.sin(angles)
    return (
        jnp.concatenate([cosine] * 4, -1),
        jnp.concatenate([-sine, sine, -sine, sine], -1),
    )


def body(
    hidden_in, cotangent, w_qkv, w_out, w_in, w_mix, attn_gain, mlp_gain, segment_ids, positions
):
    seqs, local, width = hidden_in.shape
    rows = seqs * local
    length = local * lax.axis_size("ctx")
    total = seqs * length
    pairs = HEADS // 2
    bf, f32 = jnp.bfloat16, jnp.float32
    place = lax.axis_index("ctx") * local

    dp_size, ctx_size = lax.axis_size("dp"), lax.axis_size("ctx")
    shard = width // dp_size
    own_gains = jnp.pad(jnp.stack([attn_gain, mlp_gain]), ((0, 30), (0, 256 - shard)))
    own_marks = jnp.pad(jnp.concatenate([segment_ids, positions]), ((0, 8 - 2 * seqs), (0, 0)))
    full_out, full_in, full_mix = (
        lax.all_gather(weight, "dp", axis=0, tiled=True) for weight in (w_out, w_in, w_mix)
    )
    full_qkv, gains, hidden_all, marks = gather(
        [w_qkv, own_gains], [hidden_in, own_marks.reshape(1, 8, local)], 0
    )
    gains = gains.reshape(dp_size, 32, 256)[:, :2, :shard]
    gains = jnp.transpose(gains, (1, 0, 2)).reshape(2, width)
    marks = marks.reshape(ctx_size, 8, local)[:, : 2 * seqs].reshape(ctx_size, 2, seqs, local)
    marks = jnp.transpose(marks, (1, 2, 0, 3)).reshape(2, seqs, length)
    gain_attn, gain_mlp = gains[0].astype(f32), gains[1].astype(f32)

    cos_all, sin_all = tables(marks[1])
    cos_own, sin_own = tables(positions)
    seg_row = marks[0]
    seg_col = jnp.broadcast_to(segment_ids.reshape(rows, 1), (rows, 128))

    inputs = hidden_in.astype(f32).reshape(rows, width)
    normed_attn, attn_norm_back = jax.vjp(norm_gain, inputs, gain_attn)
    x_own = normed_attn.astype(bf)
    x_all = norm_gain(hidden_all.astype(f32).reshape(total, width), gain_attn).astype(bf)

    def const(*shape):
        return pl.BlockSpec(shape, lambda pair: (0,) * len(shape))

    def column(height, offset=0):
        return pl.BlockSpec((height, PAIR), lambda pair: (0, pair + offset))

    shared = [
        const(total, width), const(rows, width),
        column(width), column(width, pairs), column(width, 2 * pairs),
        const(total, PAIR), const(total, PAIR), const(rows, PAIR), const(rows, PAIR),
        const(rows, 128), const(seqs, length),
    ]
    shared_args = (
        x_all, x_own, full_qkv, full_qkv, full_qkv, cos_all, sin_all, cos_own, sin_own, seg_col, seg_row
    )
    params = pltpu.CompilerParams(vmem_limit_bytes=VMEM_LIMIT)
    score_flops = 2 * rows * length * PAIR * HEADS
    q_own, k_all, v_all, attention, logs = pl.pallas_call(
        lambda *refs: forward_kernel(seqs, *refs),
        grid=(pairs,),
        in_specs=shared,
        out_specs=[column(rows), column(total), column(total), column(rows), column(rows)],
        out_shape=[
            jax.ShapeDtypeStruct((rows, width), bf),
            jax.ShapeDtypeStruct((total, width), bf),
            jax.ShapeDtypeStruct((total, width), bf),
            jax.ShapeDtypeStruct((rows, width), f32),
            jax.ShapeDtypeStruct((rows, width), f32),
        ],
        compiler_params=params,
        cost_estimate=pl.CostEstimate(
            flops=2 * score_flops + 4 * total * width * width,
            bytes_accessed=20 * 1024 * 1024, transcendentals=rows * length * HEADS,
        ),
    )(*shared_args)

    attn_low = attention.astype(bf)
    residual = inputs + dot_nn(attn_low, full_out)
    normed_mlp, mlp_norm_back = jax.vjp(norm_gain, residual, gain_mlp)
    mlp_low = normed_mlp.astype(bf)
    wide_proj = dot_nn(mlp_low, full_in)
    activated, geglu_back = jax.vjp(geglu, wide_proj)
    act_low = activated.astype(bf)
    output = residual + dot_nn(act_low, full_mix)
    grad_out = cotangent.reshape(rows, width)
    grad_mix = inner(act_low, grad_out).astype(bf)
    grad_wide = geglu_back(times_back(grad_out, full_mix))[0].astype(bf)
    grad_in = inner(mlp_low, grad_wide).astype(bf)
    grad_norm_in, grad_gain_mlp = mlp_norm_back(times_back(grad_wide, full_in))
    grad_resid = grad_out.astype(f32) + grad_norm_in
    grad_branch = grad_resid.astype(bf)
    grad_attn_out = inner(attn_low, grad_branch).astype(bf)
    g_own = times_back(grad_branch, full_out).astype(bf)

    feature = lax.broadcasted_iota(jnp.int32, (width, HEADS), 0)
    head = lax.broadcasted_iota(jnp.int32, (width, HEADS), 1)
    members = (feature // HEAD_DIM == head).astype(f32)
    opening = (feature == head * HEAD_DIM).astype(f32)
    highest = lax.Precision.HIGHEST
    stats = jnp.concatenate(
        [
            jnp.dot(logs, opening, precision=highest),
            jnp.dot(g_own.astype(f32) * attention, members, precision=highest),
        ],
        -1,
    )
    upper = lax.reduce_precision(stats, 8, 7)
    middle = lax.reduce_precision(stats - upper, 8, 7)
    lower = stats - upper - middle
    packed = jnp.concatenate(
        [g_own, upper.astype(bf), middle.astype(bf), lower.astype(bf), jnp.zeros((rows, 128 - 6 * HEADS), bf)], -1
    )
    (arrived,) = gather([], [packed.reshape(seqs, local, width + 128)], 1)
    pieces = arrived[..., width : width + 6 * HEADS].astype(f32)
    pieces = pieces[..., : 2 * HEADS] + pieces[..., 2 * HEADS : 4 * HEADS] + pieces[..., 4 * HEADS :]
    rows_view = jnp.transpose(pieces.reshape(seqs, length, 2, pairs, 2), (2, 3, 0, 4, 1)).reshape(
        2, pairs, 2 * seqs, length
    )
    k_own = lax.dynamic_slice(k_all.reshape(seqs, length, width), (0, place, 0), (seqs, local, width))
    v_own = lax.dynamic_slice(v_all.reshape(seqs, length, width), (0, place, 0), (seqs, local, width))
    stat_spec = pl.BlockSpec((1, 2 * seqs, length), lambda pair: (pair, 0, 0))
    dw_qkv, back = pl.pallas_call(
        lambda *refs: backward_kernel(seqs, *refs),
        grid=(pairs,),
        in_specs=shared
        + [column(rows)] * 3
        + [column(total)] * 2
        + [column(rows), column(total), column(rows), column(rows), stat_spec, stat_spec],
        out_specs=[
            pl.BlockSpec((3, width, PAIR), lambda pair: (0, 0, pair)),
            const(rows, width),
        ],
        out_shape=[
            jax.ShapeDtypeStruct((3, width, width), bf),
            jax.ShapeDtypeStruct((rows, width), f32),
        ],
        scratch_shapes=[pltpu.VMEM((total, PAIR), bf), pltpu.VMEM((3, rows, PAIR), bf)],
        compiler_params=params,
        cost_estimate=pl.CostEstimate(
            flops=7 * score_flops + 2 * total * width * width + 12 * rows * width * width,
            bytes_accessed=25 * 1024 * 1024, transcendentals=2 * rows * length * HEADS,
        ),
    )(
        *shared_args, q_own, k_own.reshape(rows, width), v_own.reshape(rows, width), k_all, v_all,
        g_own, arrived.reshape(total, width + 128), attention, logs, rows_view[0], rows_view[1],
    )
    grad_norm_attn, grad_gain_attn = attn_norm_back(back)
    grad_hidden = (grad_resid + grad_norm_attn).astype(bf).reshape(hidden_in.shape)

    def by_owner(term):
        return term.reshape(dp_size, -1, width)

    def thirds(term):
        parts = [by_owner(term[..., part * width : (part + 1) * width]) for part in range(3)]
        return parts

    gain_rows = jnp.stack([grad_gain_attn, grad_gain_mlp]).reshape(2, dp_size, shard)
    gain_rows = jnp.pad(jnp.transpose(gain_rows, (1, 0, 2)), ((0, 0), (0, 0), (0, width - shard)))
    early = jnp.concatenate(thirds(grad_in) + [by_owner(grad_attn_out), by_owner(grad_mix)], 1)
    early = lax.psum_scatter(early, "dp", scatter_dimension=0, tiled=True)
    stacked = [by_owner(dw_qkv[part]) for part in range(3)]
    used = 3 * shard
    padded = -(-(used + 2) // 128) * 128
    stacked.append(jnp.pad(gain_rows.astype(bf), ((0, 0), (0, padded - used - 2), (0, 0))))
    early, late = lax.optimization_barrier((early, jnp.concatenate(stacked, 1)))
    early = lax.psum(early, "ctx")[0].astype(f32)
    summed = reduce_terms(late, 2).astype(f32)
    cuts = [early[part * shard : (part + 1) * shard] for part in range(4)]
    return (
        output.astype(bf).reshape(hidden_in.shape),
        grad_hidden,
        jnp.concatenate([summed[part * shard : (part + 1) * shard] for part in range(3)], 1),
        cuts[3],
        jnp.concatenate(cuts[:3], 1),
        early[4 * shard :],
        summed[used, :shard],
        summed[used + 1, :shard],
    )


def layer(hidden_in, *others):
    sizes = (lax.axis_size("dp"), lax.axis_size("ctx"))
    if sizes != (4, 8) or hidden_in.shape[0] * hidden_in.shape[1] * sizes[1] > 4096:
        return long_body(hidden_in, *others)
    return body(hidden_in, *others)


def solution(mesh):
    placed = (
        P("dp", "ctx", None),
        P("dp", "ctx", None),
        P("dp", None),
        P("dp", None),
        P("dp", None),
        P("dp", None),
        P("dp"),
        P("dp"),
        P("dp", "ctx"),
        P("dp", "ctx"),
    )
    return jax.shard_map(
        layer,
        mesh=mesh,
        in_specs=placed,
        out_specs=(
            P("dp", "ctx", None),
            P("dp", "ctx", None),
            P("dp", None),
            P("dp", None),
            P("dp", None),
            P("dp", None),
            P("dp"),
            P("dp"),
        ),
        check_vma=False,
    )
```
